256 devices in a mesh: dp: 16 (over z_hi, y), tensor: 8 (over z_lo, x), probe: 2 (over core).
Axes of the slice: x: 4, y: 4, z: 8 (z_hi: 4, z_lo: 2; z = z_hi * 2 + z_lo), core: 2. Of those that a mesh axis runs over, the one named last changes fastest.
Arguments:
- tokens: bfloat16 [2048, 4096], P('dp'), may hold values from -6 to 6
- cotangent: bfloat16 [2048, 4096], P('dp'), may hold values from -6 to 6
- gate_weight: bfloat16 [4096, 14336], P('dp', ('tensor', 'probe')), may hold values from -0.09375 to 0.09375
- up_weight: bfloat16 [4096, 14336], P('dp', ('tensor', 'probe')), may hold values from -0.09375 to 0.09375
- down_weight: bfloat16 [14336, 4096], P(('tensor', 'probe'), 'dp'), may hold values from -0.046875 to 0.046875
- probe_seeds: int32 [2], replicated, may hold values from 0 to 1073741823
Outputs:
- tangent: bfloat16 [2, 2048, 4096], P(None, 'dp', ('tensor', 'probe'))
- curvature: float32 [2, 2048], P(None, 'dp')
The draws below stay inside these ranges and needn't reach their ends.
Inputs may be any that keep to these rules, and one draw needn't show every extreme that they name: `probe_seeds`: seeds of the probes; the signs are the fixed function of them given in the reference program.
All inputs are finite; a program needn't handle non-finite values.
Results may differ from the reference program's by a relative error of at most 0.023.
Values may be sent and summed in bfloat16 or wider, within the bound.
A program may use at most 128 MiB of HBM per device.

```python
import jax
import jax.numpy as jnp
from jax import lax

D = 4096
FF = 14336
PROBES = 2
TOKENS = 2048
N_TENSOR = 8
N_PROBE = 2


def block_scale(key, shape, pieces, low, top_value):
    gain, own = 1.0, jax.random.fold_in(key, 6)
    for dim, blocks in pieces:
        draws = jnp.exp(jax.random.uniform(jax.random.fold_in(own, dim), (blocks,), jnp.float32, low / len(pieces), top_value / len(pieces)))
        gain = gain * jnp.repeat(draws, shape[dim] // blocks).reshape([-1 if axis == dim else 1 for axis in range(len(shape))])
    return gain


def scatter_about(rng, dims, width, limit, cuts=(), held_as=jnp.bfloat16):
    level = block_scale(rng, dims, cuts, -0.22, 0.18) if cuts else 1.0
    array = jax.random.normal(rng, dims, jnp.float32) * width * level
    return jnp.minimum(jnp.maximum(array, -limit), limit).astype(held_as)


def setup_inputs(seed: int = 0) -> dict:
    splits = jax.random.split(jax.random.key(seed), 7)
    tokens = scatter_about(splits[0], (TOKENS, D), 1.0, 6.0, ((0, 16),))
    cotangent = scatter_about(splits[1], (TOKENS, D), 1.0, 6.0, ((0, 16),))
    gate_weight = scatter_about(splits[2], (D, FF), D ** -0.5, 0.09375, ((0, 16), (1, 16)))
    up_weight = scatter_about(splits[3], (D, FF), D ** -0.5, 0.09375, ((0, 16), (1, 16)))
    down_weight = scatter_about(splits[4], (FF, D), FF ** -0.5, 0.046875, ((0, 16), (1, 16)))
    probe_seeds = jax.random.randint(splits[5], (PROBES,), 0, 1073741824).astype(jnp.int32)
    return {"tokens": tokens, "cotangent": cotangent, "gate_weight": gate_weight, "up_weight": up_weight, "down_weight": down_weight, "probe_seeds": probe_seeds}


def upper_bits(number, shift_by):
    return jnp.right_shift(number, shift_by) & ((1 << (32 - shift_by)) - 1)


def rademacher(seed_value, salt, row_ids, col_ids, col_total, factor):
    flat_index = row_ids[:, None] * col_total + col_ids[None, :]
    hashed = flat_index * jnp.int32(-1640531535) + (seed_value + salt * 40503)
    hashed = hashed ^ upper_bits(hashed, 16)
    hashed = hashed * jnp.int32(739982445)
    hashed = hashed ^ upper_bits(hashed, 13)
    hashed = hashed * jnp.int32(695872825)
    hashed = hashed ^ upper_bits(hashed, 16)
    signs = 1 - 2 * upper_bits(hashed, 31)
    return (signs.astype(jnp.float32) * factor).astype(jnp.bfloat16)


def silu_terms(gate_pre):
    sigmoid_val = jax.nn.sigmoid(gate_pre)
    silu_val = gate_pre * sigmoid_val
    silu_slope = sigmoid_val * (1.0 + gate_pre * (1.0 - sigmoid_val))
    silu_bend = sigmoid_val * (1.0 - sigmoid_val) * (2.0 + gate_pre * (1.0 - 2.0 * sigmoid_val))
    return silu_val, silu_slope, silu_bend


def reference(tokens, cotangent, gate_weight, up_weight, down_weight, probe_seeds):
    in_factor = D ** -0.5
    out_factor = FF ** -0.5
    feature_ids = jnp.arange(D, dtype=jnp.int32)
    unit_ids = jnp.arange(FF, dtype=jnp.int32)
    gate_pre = jnp.dot(tokens, gate_weight, preferred_element_type=jnp.float32)
    up_pre = jnp.dot(tokens, up_weight, preferred_element_type=jnp.float32)
    gate_list, up_list, down_dirs = [], [], []
    for probe_index in range(PROBES):
        seed_value = probe_seeds[probe_index]
        gate_list.append(jnp.dot(tokens, rademacher(seed_value, 1, feature_ids, unit_ids, FF, in_factor), preferred_element_type=jnp.float32))
        up_list.append(jnp.dot(tokens, rademacher(seed_value, 2, feature_ids, unit_ids, FF, in_factor), preferred_element_type=jnp.float32))
        down_dirs.append(rademacher(seed_value, 3, unit_ids, feature_ids, D, out_factor))
    gate_dir = jnp.stack(gate_list)
    up_dir = jnp.stack(up_list)
    silu_val, silu_slope, silu_bend = silu_terms(gate_pre)
    hidden = (silu_val * up_pre).astype(jnp.bfloat16)
    hidden_dir = silu_slope * gate_dir * up_pre + silu_val * up_dir
    hidden_dir_low = hidden_dir.astype(jnp.bfloat16)
    hidden_curv = silu_bend * gate_dir * gate_dir * up_pre + 2.0 * silu_slope * gate_dir * up_dir
    back_plain = jnp.dot(cotangent, down_weight.T, preferred_element_type=jnp.float32)
    back_dir = jnp.stack([jnp.dot(cotangent, down_dirs[k].T, preferred_element_type=jnp.float32) for k in range(PROBES)])
    curvature = jnp.sum(back_plain[None] * hidden_curv + 2.0 * back_dir * hidden_dir, axis=2) * out_factor
    block_size = FF // (N_TENSOR * N_PROBE)
    tangent_list = []
    for probe_index in range(PROBES):
        running = jnp.zeros((tokens.shape[0], D), jnp.float32)
        for block_index in range(N_TENSOR * N_PROBE):
            lower = block_index * block_size
            upper = lower + block_size
            partial_sum = jnp.dot(hidden_dir_low[probe_index][:, lower:upper], down_weight[lower:upper], preferred_element_type=jnp.float32)
            partial_sum = partial_sum + jnp.dot(hidden[:, lower:upper], down_dirs[probe_index][lower:upper], preferred_element_type=jnp.float32)
            running = running + lax.optimization_barrier(partial_sum.astype(jnp.bfloat16)).astype(jnp.float32)
        tangent_list.append(running.astype(jnp.bfloat16))
    tangent = jnp.stack(tangent_list)
    return tangent, curvature
```

```python
import functools

import jax
import jax.numpy as jnp
import numpy as np
from jax import lax
from jax.experimental import pallas as pl
from jax.experimental.pallas import tpu as pltpu
from jax.sharding import PartitionSpec as P

D = 4096
FF = 14336
UNITS = 224
COLS = 256
BLOCK = 128
MESH = pl.DeviceIdType.MESH
NT = (((1,), (1,)), ((), ()))
BF16, F32, I32 = jnp.bfloat16, jnp.float32, jnp.int32
IN_FACTOR = float(D**-0.5)
OUT_FACTOR = float(FF**-0.5)
OUT_FACTOR_LOW = float(np.asarray(FF**-0.5, np.float32).astype(jnp.bfloat16))
PARTS = ((0, 2 * UNITS), (2 * UNITS, UNITS))


def wrap(value):
    return np.int32((int(value) + 2**31) % 2**32 - 2**31)


STEP = -1640531535


def kernel(
    seeds, tok, cot, wa, out, curv,
    tc, w, dirs, acc, hid, cs, cr, xs, xr, zs, zr, cv, cvc, cvx, cvz,
    loc_sem, a2a_s, a2a_r, ag_s, ag_r, tz_s, tz_r, tx_s, tx_r, tcc_s, tcc_r,
    c_s, c_r, x_s, x_r, z_s, z_r, vc_s, vc_r, vx_s, vx_r, vz_s, vz_r,
):
    dp, tensor, core = lax.axis_index("dp"), lax.axis_index("tensor"), lax.axis_index("probe")
    zh, y = dp // 4, dp % 4
    zl, x = tensor // 4, tensor % 4

    def dev_z(step):
        z = (zh * 2 + zl + step) % 8
        return ((z // 2) * 4 + y, (z % 2) * 4 + x, core)

    def dev_y(step):
        return (zh * 4 + (y + step) % 4, tensor, core)

    def dev_x(step):
        return (dp, zl * 4 + (x + step) % 4, core)

    dev_c = (dp, tensor, 1 - core)

    def remote(src, dst, send, recv, device):
        return pltpu.make_async_remote_copy(
            src_ref=src, dst_ref=dst, send_sem=send, recv_sem=recv,
            device_id=device, device_id_type=MESH,
        )

    barrier = pltpu.get_barrier_semaphore()
    peers = [dev_z(d) for d in range(1, 8)] + [dev_x(d) for d in range(1, 4)] + [dev_y(1), dev_y(3), dev_c]
    for peer in peers:
        pl.semaphore_signal(barrier, inc=1, device_id=peer, device_id_type=MESH)
    pl.semaphore_wait(barrier, len(peers))

    started = []

    def go(copy):
        copy.start()
        started.append(copy)

    def w_at(part, yy, j):
        lo, n = PARTS[part]
        return w.at[yy % 4, (zh + j) % 4, pl.ds(lo, n)]

    def ag_send(part, j):
        lo, n = PARTS[part]
        src = wa.at[zh, pl.ds(lo, n)] if j == 0 else w_at(part, y, j)
        go(remote(src, w_at(part, y, j), ag_s.at[part, j, 0], ag_r.at[part, j, 0], dev_y(1)))
        go(remote(src, w_at(part, y, j), ag_s.at[part, j, 1], ag_r.at[part, j, 1], dev_y(3)))

    def ag_wait(part, j, side, source):
        ref = w_at(part, source, j)
        remote(ref, ref, ag_s.at[part, j, side], ag_r.at[part, j, side], dev_y(1)).wait_recv()

    def ag_relay(part, j):
        side, source, onward = (0, y + 3, 1) if j % 2 == 0 else (1, y + 1, 3)
        ag_wait(part, j, side, source)
        ref = w_at(part, source, j)
        go(remote(ref, ref, ag_s.at[part, j, 2], ag_r.at[part, j, 2], dev_y(onward)))

    def ag_finish(part, j):
        side, source = (1, y + 1) if j % 2 == 0 else (0, y + 3)
        ag_wait(part, j, side, source)
        ag_wait(part, j, 2, y + 2)

    def a2a_send(part, d):
        lo, n = PARTS[part]
        target = (zh + d) % 4
        go(remote(wa.at[target, pl.ds(lo, n)], w_at(part, y, 0), a2a_s.at[part, d - 1], a2a_r.at[part, 3 - d], dev_z(2 * d)))

    def a2a_wait(part, j):
        ref = w_at(part, y, j)
        remote(ref, ref, a2a_s.at[part, j - 1], a2a_r.at[part, j - 1], dev_z(2)).wait_recv()

    def tok_send(d):
        for m, src in enumerate((tok, cot)):
            go(remote(src.at[x, core], tc.at[m, zh, x, core], tz_s.at[m, d - 1], tz_r.at[m, 3 - d], dev_z(2 * d)))

    def tok_forward(j):
        zz = (zh + j) % 4
        for m in range(2):
            ref = tc.at[m, zz, x, core]
            remote(ref, ref, tz_s.at[m, j - 1], tz_r.at[m, j - 1], dev_z(2)).wait_recv()
        ref = tc.at[:, zz, x, core]
        for e in range(1, 4):
            go(remote(ref, ref, tx_s.at[j - 1, e - 1], tx_r.at[j - 1, e - 1], dev_x(e)))

    def tok_share(j):
        zz = (zh + j) % 4
        for e in range(1, 4):
            ref = tc.at[:, zz, (x - e) % 4, core]
            remote(ref, ref, tx_s.at[j - 1, e - 1], tx_r.at[j - 1, e - 1], dev_x(1)).wait_recv()
        ref = tc.at[:, zz, :, core]
        go(remote(ref, ref, tcc_s.at[j - 1], tcc_r.at[j - 1], dev_c))

    def tok_finish(j):
        ref = tc.at[:, (zh + j) % 4, :, 1 - core]
        remote(ref, ref, tcc_s.at[j - 1], tcc_r.at[j - 1], dev_c).wait_recv()

    ag_send(0, 0)
    a2a_send(0, 1)
    a2a_send(0, 3)
    tok_send(1)
    tok_send(3)
    a2a_send(0, 2)
    tok_send(2)
    a2a_send(1, 1)
    a2a_send(1, 3)
    a2a_send(1, 2)
    ag_send(1, 0)
    local = [
        pltpu.make_async_copy(tok, tc.at[0, zh], loc_sem.at[0]),
        pltpu.make_async_copy(cot, tc.at[1, zh], loc_sem.at[1]),
        pltpu.make_async_copy(wa.at[zh], w.at[y, zh], loc_sem.at[2]),
    ]
    for copy in local:
        copy.start()

    first_unit = (tensor * 2 + core) * (4 * UNITS) + zh * UNITS

    def make_signs(m):
        unit_mul, feature_mul = (wrap(STEP), wrap(STEP * FF)) if m < 2 else (wrap(STEP * D), wrap(STEP))
        base = (
            lax.broadcasted_iota(I32, (16, D), 0) * unit_mul + lax.broadcasted_iota(I32, (16, D), 1) * feature_mul
        )

        def body(i, _):
            start = (first_unit + i * 16) * unit_mul + np.int32(40503 * (m + 1))
            for p in range(2):
                u = base + (start + seeds[p])
                u = u ^ lax.shift_right_logical(u, np.int32(16))
                u = u * np.int32(739982445)
                u = u ^ lax.shift_right_logical(u, np.int32(13))
                u = u * np.int32(695872825)
                dirs[2 * m + p, pl.ds(pl.multiple_of(i * 16, 16), 16), :] = jnp.where(u < 0, -1.0, 1.0).astype(BF16)
            return 0

        lax.fori_loop(0, UNITS // 16, body, 0)

    make_signs(0)
    ag_relay(0, 0)
    make_signs(1)
    ag_relay(1, 0)
    for j in (1, 3):
        a2a_wait(0, j)
        ag_send(0, j)
    make_signs(2)
    for j in (1, 3):
        tok_forward(j)
    for j in (1, 3):
        ag_relay(0, j)
    a2a_wait(0, 2)
    ag_send(0, 2)
    tok_forward(2)
    for j in (1, 3):
        a2a_wait(1, j)
        ag_send(1, j)
    for j in (1, 3):
        tok_share(j)
    ag_relay(0, 2)
    a2a_wait(1, 2)
    ag_send(1, 2)
    tok_share(2)
    for j in (1, 3, 2):
        tok_finish(j)
    for copy in local:
        copy.wait()
    for j in (1, 3):
        ag_relay(1, j)

    def rows_of(m, lo, n):
        return tc[m, pl.ds(lo, n)].reshape(n * BLOCK, D)

    def dir_body(i, _):
        acc[i] = lax.dot_general(rows_of(i // 4, 0, 4), dirs[i], NT, preferred_element_type=F32)
        return 0

    lax.fori_loop(0, 6, dir_body, 0)
    ag_relay(1, 2)
    for j in (0, 1, 3, 2):
        ag_finish(0, j)

    def gate_rows(i):
        return w[:, :, pl.ds(i * UNITS, UNITS), :]

    def plain(i):
        def body(b, total):
            yy, zz = b // 4, b % 4
            col = pl.ds(pl.multiple_of((zz * 4 + yy) * COLS, COLS), COLS)
            lhs = tc[i // 2, :, :, :, :, col].reshape(4 * BLOCK, COLS)
            return total + lax.dot_general(
                lhs, w[yy, zz, pl.ds(i * UNITS, UNITS), :], NT, preferred_element_type=F32
            )

        acc[6 + i] = lax.fori_loop(0, 16, body, jnp.zeros((4 * BLOCK, UNITS), F32))

    plain(0)
    plain(1)

    def point(i, _):
        r = pl.ds(pl.multiple_of(i * 32, 32), 32)
        gate, up = acc[6, r, :], acc[7, r, :]
        s = jax.nn.sigmoid(gate)
        silu = gate * s
        slope = s * (1.0 + gate * (1.0 - s))
        bend = s * (1.0 - s) * (2.0 + gate * (1.0 - 2.0 * s))
        hid[2, r, :] = (silu * up).astype(BF16)
        for p in range(2):
            gd, ud = acc[p, r, :] * IN_FACTOR, acc[2 + p, r, :] * IN_FACTOR
            hd = slope * gd * up + silu * ud
            hid[p, r, :] = hd.astype(BF16)
            acc[2 + p, r, :] = hd
            acc[p, r, :] = bend * gd * gd * up + 2.0 * slope * gd * ud
        return 0

    lax.fori_loop(0, 16, point, 0)
    for j in (0, 1, 3, 2):
        ag_finish(1, j)
    plain(2)

    cv[0] = jnp.zeros((8, 4 * BLOCK), F32)
    for p in range(2):
        terms = acc[8] * acc[p] + (2.0 * OUT_FACTOR_LOW) * acc[4 + p] * acc[2 + p]
        cv[0, pl.ds(p, 1), :] = jnp.sum(terms.T, axis=0, keepdims=True) * OUT_FACTOR
    go(remote(cv.at[0], cvc, vc_s.at[0], vc_r.at[0], dev_c))

    def columns(e, lr, other):
        return (((zl + lr) % 2) * 4 + (x + e) % 4) * 2 + other

    def tangent(p, b):
        col = pl.ds(pl.multiple_of(b * COLS, COLS), COLS)
        one = jnp.dot(hid[p], w[b % 4, b // 4, pl.ds(2 * UNITS, UNITS), :], preferred_element_type=F32)
        two = jnp.dot(hid[2], dirs[4 + p, :, col], preferred_element_type=F32)
        return one + two * OUT_FACTOR_LOW

    ORDER = (2, 1, 3, 0)

    def give(e, lr):
        k = e * 2 + lr
        return remote(cs.at[k], cr.at[k], c_s.at[k], c_r.at[k], dev_c)

    def x_copy(e, lr):
        return remote(xs.at[e, lr], xr.at[e - 1, lr], x_s.at[e - 1, lr], x_r.at[e - 1, lr], dev_x(e))

    for e in ORDER:

        def body(lr, _, e=e):
            def probe(p, _):
                cs[e * 2 + lr, p] = tangent(p, columns(e, lr, 1 - core)).astype(BF16)
                return 0

            lax.fori_loop(0, 2, probe, 0)
            give(e, lr).start()

            def probe2(p, _):
                xs[e, lr, p] = tangent(p, columns(e, lr, core)).astype(BF16)
                return 0

            lax.fori_loop(0, 2, probe2, 0)
            give(e, lr).wait_recv()

            def merge(i, _):
                r = pl.ds(pl.multiple_of(i * 64, 64), 64)
                for p in range(2):
                    xs[e, lr, p, r, :] = (
                        xs[e, lr, p, r, :].astype(F32) + cr[e * 2 + lr, p, r, :].astype(F32)
                    ).astype(BF16)
                return 0

            lax.fori_loop(0, 8, merge, 0)
            if e:
                x_copy(e, lr).start()
            return 0

        lax.fori_loop(0, 2, body, 0)
        if e == 1:
            ref = cvc
            remote(ref, ref, vc_s.at[0], vc_r.at[0], dev_c).wait_recv()
            cv[1] = cv[0] + cvc[...]
            for d in range(1, 4):
                go(remote(cv.at[1], cvx.at[d - 1], vx_s.at[d - 1], vx_r.at[d - 1], dev_x(d)))
        if e == 0:
            for d in range(1, 4):
                remote(cv.at[1], cvx.at[d - 1], vx_s.at[d - 1], vx_r.at[d - 1], dev_x(d)).wait_recv()
            cv[2] = (cv[1] + cvx[0]) + (cvx[1] + cvx[2])
            for d in range(1, 8):
                zz = ((zh * 2 + zl + d) % 8) // 2
                src = cv.at[2, :, pl.ds(pl.multiple_of(zz * BLOCK, BLOCK), BLOCK)]
                go(remote(src, cvz.at[d - 1], vz_s.at[d - 1], vz_r.at[d - 1], dev_z(d)))

    def z_copy(d, lr):
        zz = ((zh * 2 + zl + d) % 8) // 2
        return remote(
            zs.at[lr, :, pl.ds(pl.multiple_of(zz * BLOCK, BLOCK), BLOCK)], zr.at[d - 1], z_s.at[d - 1], z_r.at[d - 1], dev_z(d)
        )

    for lr, steps in ((1, (1, 7, 3, 5)), (0, (2, 6, 4))):
        for e in (1, 3, 2):
            x_copy(e, lr).wait_recv()

        def merge(i, _, lr=lr):
            r = pl.ds(pl.multiple_of(i * 64, 64), 64)
            for p in range(2):
                total = xs[0, lr, p, r, :].astype(F32)
                for e in range(3):
                    total = total + xr[e, lr, p, r, :].astype(F32)
                zs[lr, p, r, :] = total.astype(BF16)
            return 0

        lax.fori_loop(0, 8, merge, 0)
        for d in steps:
            go(z_copy(d, lr))

    for d in range(1, 8):
        remote(cvz.at[d - 1], cvz.at[d - 1], vz_s.at[d - 1], vz_r.at[d - 1], dev_z(d)).wait_recv()
    total = cv[2, :, pl.ds(pl.multiple_of(zh * BLOCK, BLOCK), BLOCK)]
    for d in range(7):
        total = total + cvz[d]
    curv[...] = total[:2]

    for d in range(1, 8):
        remote(zr.at[d - 1], zr.at[d - 1], z_s.at[d - 1], z_r.at[d - 1], dev_z(d)).wait_recv()

    def last(i, _):
        r = pl.ds(pl.multiple_of(i * 32, 32), 32)
        own = pl.ds(pl.multiple_of(zh * BLOCK + i * 32, 32), 32)
        for p in range(2):
            total = zs[0, p, own, :].astype(F32)
            for d in range(7):
                total = total + zr[d, p, r, :].astype(F32)
            out[p, r, :] = total.astype(BF16)
        return 0

    lax.fori_loop(0, 4, last, 0)
    for copy in started:
        copy.wait_send()
    for e in ORDER:
        for lr in range(2):
            give(e, lr).wait_send()
            if e:
                x_copy(e, lr).wait_send()


def on_device(tokens, cotangent, gate_weight, up_weight, down_weight, probe_seeds):
    weights = jnp.concatenate(
        [part.reshape(4, UNITS, COLS) for part in (gate_weight.T, up_weight.T, down_weight)], axis=1
    )
    dma = pltpu.SemaphoreType.DMA
    vmem = pltpu.VMEM
    hbm = pl.BlockSpec(memory_space=pl.ANY)
    tangent, curvature = pl.pallas_call(
        kernel,
        out_shape=(
            jax.ShapeDtypeStruct((2, BLOCK, COLS), BF16),
            jax.ShapeDtypeStruct((2, BLOCK), F32),
        ),
        in_specs=[pl.BlockSpec(memory_space=pltpu.SMEM), hbm, hbm, hbm],
        out_specs=(pl.BlockSpec(memory_space=pltpu.VMEM), pl.BlockSpec(memory_space=pltpu.VMEM)),
        scratch_shapes=[
            vmem((2, 4, 4, 2, 16, D), BF16),
            vmem((4, 4, 3 * UNITS, COLS), BF16),
            vmem((6, UNITS, D), BF16),
            vmem((9, 4 * BLOCK, UNITS), F32),
            vmem((3, 4 * BLOCK, UNITS), BF16),
            vmem((8, 2, 4 * BLOCK, COLS), BF16),
            vmem((8, 2, 4 * BLOCK, COLS), BF16),
            vmem((4, 2, 2, 4 * BLOCK, COLS), BF16),
            vmem((3, 2, 2, 4 * BLOCK, COLS), BF16),
            vmem((2, 2, 4 * BLOCK, COLS), BF16),
            vmem((7, 2, BLOCK, COLS), BF16),
            vmem((3, 8, 4 * BLOCK), F32),
            vmem((8, 4 * BLOCK), F32),
            vmem((3, 8, 4 * BLOCK), F32),
            vmem((7, 8, BLOCK), F32),
            dma((3,)),
            dma((2, 3)), dma((2, 3)),
            dma((2, 4, 3)), dma((2, 4, 3)),
            dma((2, 3)), dma((2, 3)),
            dma((3, 3)), dma((3, 3)),
            dma((3,)), dma((3,)),
            dma((8,)), dma((8,)),
            dma((3, 2)), dma((3, 2)),
            dma((7,)), dma((7,)),
            dma((1,)), dma((1,)),
            dma((3,)), dma((3,)),
            dma((7,)), dma((7,)),
        ],
        name="curvature_probes",
        cost_estimate=pl.CostEstimate(flops=13 * 2 * 512 * D * UNITS, bytes_accessed=4 * 2**20, transcendentals=512 * UNITS),
        compiler_params=pltpu.CompilerParams(
            collective_id=0, has_side_effects=True, vmem_limit_bytes=60 * 2**20
        ),
    )(
        probe_seeds,
        tokens.reshape(4, 2, 16, D),
        cotangent.reshape(4, 2, 16, D),
        weights,
    )
    return tangent, curvature


def solution(mesh):
    return jax.shard_map(
        on_device,
        mesh=mesh,
        in_specs=(
            P("dp", None),
            P("dp", None),
            P("dp", ("tensor", "probe")),
            P("dp", ("tensor", "probe")),
            P(("tensor", "probe"), "dp"),
            P(),
        ),
        out_specs=(P(None, "dp", ("tensor", "probe")), P(None, "dp")),
        check_vma=False,
    )
```

```python
import functools

import jax
import jax.numpy as jnp
import numpy as np
from jax import lax
from jax.experimental import pallas as pl
from jax.experimental.pallas import tpu as pltpu
from jax.sharding import PartitionSpec as P

D = 4096
FF = 14336
UNITS = 224
COLS = 256
BLOCK = 128
MESH = pl.DeviceIdType.MESH
NT = (((1,), (1,)), ((), ()))
BF16, F32, I32 = jnp.bfloat16, jnp.float32, jnp.int32
IN_FACTOR = float(D**-0.5)
OUT_FACTOR = float(FF**-0.5)
OUT_FACTOR_LOW = float(np.asarray(FF**-0.5, np.float32).astype(jnp.bfloat16))
PARTS = ((0, 2 * UNITS), (2 * UNITS, UNITS))


def wrap(value):
    return np.int32((int(value) + 2**31) % 2**32 - 2**31)


STEP = -1640531535


def kernel(
    seeds, tok, cot, wa, out, curv,
    tc, w, dirs, acc, hid, cs0, cr0, s0, xr0, zr0, cs1, cr1, s1, zr1, xr1, cv, cvc, cvx, cvz,
    loc_sem, a2a_s, a2a_r, ag_s, ag_r, tz_s, tz_r, tx_s, tx_r, tcc_s, tcc_r,
    c_s, c_r, x0_s, x0_r, z0_s, z0_r, z1_s, z1_r, x1_s, x1_r, vc_s, vc_r, vx_s, vx_r, vz_s, vz_r,
):
    dp, tensor, core = lax.axis_index("dp"), lax.axis_index("tensor"), lax.axis_index("probe")
    zh, y = dp // 4, dp % 4
    zl, x = tensor // 4, tensor % 4

    def dev_z(step):
        z = (zh * 2 + zl + step) % 8
        return ((z // 2) * 4 + y, (z % 2) * 4 + x, core)

    def dev_y(step):
        return (zh * 4 + (y + step) % 4, tensor, core)

    def dev_x(step):
        return (dp, zl * 4 + (x + step) % 4, core)

    dev_c = (dp, tensor, 1 - core)

    def remote(src, dst, send, recv, device):
        return pltpu.make_async_remote_copy(
            src_ref=src, dst_ref=dst, send_sem=send, recv_sem=recv,
            device_id=device, device_id_type=MESH,
        )

    barrier = pltpu.get_barrier_semaphore()
    peers = [dev_z(d) for d in range(1, 8)] + [dev_x(d) for d in range(1, 4)] + [dev_y(1), dev_y(3), dev_c]
    for peer in peers:
        pl.semaphore_signal(barrier, inc=1, device_id=peer, device_id_type=MESH)
    pl.semaphore_wait(barrier, len(peers))

    started = []

    def go(copy):
        copy.start()
        started.append(copy)

    def w_at(part, yy, j):
        lo, n = PARTS[part]
        return w.at[yy % 4, (zh + j) % 4, pl.ds(lo, n)]

    def ag_send(part, j):
        lo, n = PARTS[part]
        src = wa.at[zh, pl.ds(lo, n)] if j == 0 else w_at(part, y, j)
        go(remote(src, w_at(part, y, j), ag_s.at[part, j, 0], ag_r.at[part, j, 0], dev_y(1)))
        go(remote(src, w_at(part, y, j), ag_s.at[part, j, 1], ag_r.at[part, j, 1], dev_y(3)))

    def ag_wait(part, j, side, source):
        ref = w_at(part, source, j)
        remote(ref, ref, ag_s.at[part, j, side], ag_r.at[part, j, side], dev_y(1)).wait_recv()

    def ag_relay(part, j):
        side, source, onward = (0, y + 3, 1) if j % 2 == 0 else (1, y + 1, 3)
        ag_wait(part, j, side, source)
        ref = w_at(part, source, j)
        go(remote(ref, ref, ag_s.at[part, j, 2], ag_r.at[part, j, 2], dev_y(onward)))

    def ag_finish(part, j):
        side, source = (1, y + 1) if j % 2 == 0 else (0, y + 3)
        ag_wait(part, j, side, source)
        ag_wait(part, j, 2, y + 2)

    def a2a_send(part, d):
        lo, n = PARTS[part]
        target = (zh + d) % 4
        go(remote(wa.at[target, pl.ds(lo, n)], w_at(part, y, 0), a2a_s.at[part, d - 1], a2a_r.at[part, 3 - d], dev_z(2 * d)))

    def a2a_wait(part, j):
        ref = w_at(part, y, j)
        remote(ref, ref, a2a_s.at[part, j - 1], a2a_r.at[part, j - 1], dev_z(2)).wait_recv()

    def tz(up, k, block, m, own=False):
        src = (tok, cot)[m].at[x, core] if own else tc.at[m, block % 4, x, core]
        side = 0 if up else 1
        return remote(src, tc.at[m, block % 4, x, core], tz_s.at[side, k], tz_r.at[side, k], dev_z(1 if up else 7))

    def tz_block(up, k):
        near = zh + 3 if up else zh + 1
        return (near, (0, 1, 0)[k] if up else (1, 0, 1)[k]) if k < 2 else (zh + 2, 0 if up else 1)

    def tz_wait(up, k):
        block, m = tz_block(up, k)
        tz(up, k, block, m).wait_recv()

    def tz_open(up):
        for k in range(2):
            m = k if up else 1 - k

            @pl.when(zl == (1 if up else 0))
            def _():
                tz(up, k, zh, m, own=True).start()

    def tz_pass(up, k):
        block, m = tz_block(up, k)

        @pl.when(zl == (0 if up else 1))
        def _():
            tz_wait(up, k)
            tz(up, k, block, m).start()

    def tz_half(up):
        @pl.when(zl == (1 if up else 0))
        def _():
            tz_wait(up, 0)
            tz(up, 2, zh + 3 if up else zh + 1, 0 if up else 1).start()

    def tz_rest(up, k):
        if k == 0:
            return

        @pl.when(zl == (1 if up else 0))
        def _():
            tz_wait(up, k)

    def tx(j, side):
        ref = tc.at[:, (zh + j) % 4, x, core]
        return remote(ref, ref, tx_s.at[j - 1, side], tx_r.at[j - 1, side], dev_x(1 if side == 0 else 3))

    def tx_send(j):
        go(tx(j, 0))
        go(tx(j, 1))

    def tx_relay(j):
        for side in range(2):
            ref = tc.at[:, (zh + j) % 4, (x + (3 if side == 0 else 1)) % 4, core]
            remote(ref, ref, tx_s.at[j - 1, side], tx_r.at[j - 1, side], dev_x(1)).wait_recv()
            ref = ref.at[side]
            go(remote(ref, ref, tx_s.at[j - 1, 2 + side], tx_r.at[j - 1, 2 + side], dev_x(1 if side == 0 else 3)))

    def tok_share(j):
        for side in range(2):
            ref = tc.at[side, (zh + j) % 4, (x + 2) % 4, core]
            remote(ref, ref, tx_s.at[j - 1, 2 + side], tx_r.at[j - 1, 2 + side], dev_x(1)).wait_recv()
        ref = tc.at[:, (zh + j) % 4, :, core]
        go(remote(ref, ref, tcc_s.at[j - 1], tcc_r.at[j - 1], dev_c))

    def tok_finish(j):
        ref = tc.at[:, (zh + j) % 4, :, 1 - core]
        remote(ref, ref, tcc_s.at[j - 1], tcc_r.at[j - 1], dev_c).wait_recv()

    tz_open(True)
    tz_open(False)
    ag_send(0, 0)
    local = [
        pltpu.make_async_copy(tok, tc.at[0, zh], loc_sem.at[0]),
        pltpu.make_async_copy(cot, tc.at[1, zh], loc_sem.at[1]),
        pltpu.make_async_copy(wa.at[zh], w.at[y, zh], loc_sem.at[2]),
    ]
    for copy in local:
        copy.start()

    first_unit = (tensor * 2 + core) * (4 * UNITS) + zh * UNITS

    def make_signs(m, lo, hi):
        unit_mul, feature_mul = (wrap(STEP), wrap(STEP * FF)) if m < 2 else (wrap(STEP * D), wrap(STEP))
        base = (
            lax.broadcasted_iota(I32, (16, D), 0) * unit_mul + lax.broadcasted_iota(I32, (16, D), 1) * feature_mul
        )

        def body(i, _):
            start = (first_unit + i * 16) * unit_mul + np.int32(40503 * (m + 1))
            for p in range(2):
                u = base + (start + seeds[p])
                u = u ^ lax.shift_right_logical(u, np.int32(16))
                u = u * np.int32(739982445)
                u = u ^ lax.shift_right_logical(u, np.int32(13))
                u = u * np.int32(695872825)
                dirs[2 * m + p, pl.ds(pl.multiple_of(i * 16, 16), 16), :] = jnp.where(u < 0, -1.0, 1.0).astype(BF16)
            return 0

        lax.fori_loop(lo, hi, body, 0)

    make_signs(0, 0, 7)
    for k in range(2):
        for up in (True, False):
            tz_pass(up, k)
        make_signs(0, 7 + 3 * k, 10 + 4 * k)
    for up in (True, False):
        tz_half(up)
    a2a_send(0, 1)
    a2a_send(0, 3)
    ag_relay(0, 0)
    ag_send(1, 0)
    make_signs(1, 0, 4)
    for up in (True, False):
        tz_rest(up, 1)
    tx_send(1)
    tx_send(3)
    make_signs(1, 4, 8)
    for up in (True, False):
        tz_pass(up, 2)
    make_signs(1, 8, 14)
    for up in (True, False):
        tz_rest(up, 2)
    tx_send(2)
    make_signs(2, 0, 3)
    for j in (1, 3):
        a2a_wait(0, j)
        ag_send(0, j)
    a2a_send(0, 2)
    ag_relay(1, 0)
    tx_relay(1)
    tx_relay(3)
    make_signs(2, 3, 14)
    tx_relay(2)
    for j in (1, 3):
        tok_share(j)
    a2a_wait(0, 2)
    ag_send(0, 2)
    for d in (1, 3, 2):
        a2a_send(1, d)
    for j in (1, 3):
        ag_relay(0, j)
    tok_share(2)
    for j in (1, 3, 2):
        tok_finish(j)
    for copy in local:
        copy.wait()

    def rows_of(m, lo, n):
        return tc[m, pl.ds(lo, n)].reshape(n * BLOCK, D)

    def dir_body(i, _):
        acc[i] = lax.dot_general(rows_of(i // 4, 0, 4), dirs[i], NT, preferred_element_type=F32)
        return 0

    lax.fori_loop(0, 3, dir_body, 0)
    for j in (1, 3):
        a2a_wait(1, j)
        ag_send(1, j)
    ag_relay(0, 2)
    lax.fori_loop(3, 6, dir_body, 0)
    a2a_wait(1, 2)
    ag_send(1, 2)
    for j in (0, 1, 3, 2):
        ag_finish(0, j)
    for j in (1, 3):
        ag_relay(1, j)

    def plain(i, _):
        rhs = jnp.concatenate([w[b % 4, b // 4, pl.ds(i * UNITS, UNITS), :] for b in range(16)], axis=1)
        acc[6 + i] = lax.dot_general(rows_of(i // 2, 0, 4), rhs, NT, preferred_element_type=F32)
        return 0

    lax.fori_loop(0, 2, plain, 0)
    ag_relay(1, 2)

    def point(i, _):
        r = pl.ds(pl.multiple_of(i * 32, 32), 32)
        gate, up = acc[6, r, :], acc[7, r, :]
        s = jax.nn.sigmoid(gate)
        silu = gate * s
        slope = s * (1.0 + gate * (1.0 - s))
        bend = s * (1.0 - s) * (2.0 + gate * (1.0 - 2.0 * s))
        hid[2, r, :] = (silu * up).astype(BF16)
        for p in range(2):
            gd, ud = acc[p, r, :] * IN_FACTOR, acc[2 + p, r, :] * IN_FACTOR
            hd = slope * gd * up + silu * ud
            hid[p, r, :] = hd.astype(BF16)
            acc[2 + p, r, :] = hd
            acc[p, r, :] = bend * gd * gd * up + 2.0 * slope * gd * ud
        return 0

    lax.fori_loop(0, 16, point, 0)
    for j in (0, 1, 3, 2):
        ag_finish(1, j)
    lax.fori_loop(2, 3, plain, 0)

    cv[0] = jnp.zeros((8, 4 * BLOCK), F32)
    for p in range(2):
        terms = acc[8] * acc[p] + (2.0 * OUT_FACTOR_LOW) * acc[4 + p] * acc[2 + p]
        cv[0, pl.ds(p, 1), :] = jnp.sum(terms.T, axis=0, keepdims=True) * OUT_FACTOR
    go(remote(cv.at[0], cvc, vc_s.at[0], vc_r.at[0], dev_c))

    def columns(e, lr, other):
        return (((zl + lr) % 2) * 4 + (x + e) % 4) * 2 + other

    def tangent(p, b):
        col = pl.ds(pl.multiple_of(b * COLS, COLS), COLS)
        one = jnp.dot(hid[p], w[b % 4, b // 4, pl.ds(2 * UNITS, UNITS), :], preferred_element_type=F32)
        two = jnp.dot(hid[2], dirs[4 + p, :, col], preferred_element_type=F32)
        return one + two * OUT_FACTOR_LOW

    def group(p, g):
        n, mine, out_ref, in_ref = (4, s1, cs1, cr1) if p else (2, s0, cs0, cr0)

        def column(i, side):
            return columns((i - x) % 4, g, side) if p else columns(g, i, side)

        def theirs(i, _):
            out_ref[g, pl.ds(i, 1)] = tangent(p, column(i, 1 - core)).astype(BF16)[None]
            return 0

        lax.fori_loop(0, n, theirs, 0)
        give = remote(out_ref.at[g], in_ref.at[g], c_s.at[p, g], c_r.at[p, g], dev_c)
        go(give)

        def ours(i, _):
            mine[g, pl.ds(i, 1)] = tangent(p, column(i, core)).astype(BF16)[None]
            return 0

        lax.fori_loop(0, n, ours, 0)
        give.wait_recv()

        def merge(i, _):
            r = pl.ds(pl.multiple_of((i % 8) * 64, 64), 64)
            mine[g, i // 8, r, :] = (mine[g, i // 8, r, :].astype(F32) + in_ref[g, i // 8, r, :].astype(F32)).astype(BF16)
            return 0

        lax.fori_loop(0, 8 * n, merge, 0)

    def z_rows(d, u):
        return pl.ds(pl.multiple_of((((zh * 2 + zl + d) % 8) // 2) * BLOCK + u * 64, 64), 64)

    def z_part(up, u, d):
        far = d if up else 8 - d
        return s1.at[far % 2, :, z_rows(far, u)]

    def z_hop(up, u, d):
        side = 0 if up else 1
        return remote(
            z_part(up, u, d), zr1.at[side, u, d - 1], z1_s.at[side, u, d - 1], z1_r.at[side, u, d - 1], dev_z(1 if up else 7)
        )

    def z_add(up, u, d):
        z_hop(up, u, d).wait_recv()
        far = (d - 1 if up else 9 - d) % 8

        def body(i, _):
            r = z_rows(far, u)
            s1[far % 2, i, r, :] = (
                s1[far % 2, i, r, :].astype(F32) + zr1[0 if up else 1, u, d - 1, i].astype(F32)
            ).astype(BF16)
            return 0

        lax.fori_loop(0, 4, body, 0)

    def z_step(d):
        for up in (True, False):
            lane = 0 if up else 1
            z_add(up, lane, d + 1)
            go(z_hop(up, lane, d))
        if d > 1:
            for up in (True, False):
                lane = 1 if up else 0
                z_add(up, lane, d)
                go(z_hop(up, lane, d - 1))

    def x_hop(up, u, d):
        side = 0 if up else 1
        e = d if up else 4 - d
        return remote(s0.at[e, u], xr0.at[side, u, d - 1], x0_s.at[side, u, d - 1], x0_r.at[side, u, d - 1], dev_x(1 if up else 3))

    def x_add(up, u, d):
        x_hop(up, u, d).wait_recv()
        e = (d - 1 if up else 5 - d) % 4

        def body(i, _):
            r = pl.ds(pl.multiple_of(i * 64, 64), 64)
            s0[e, u, r, :] = (s0[e, u, r, :].astype(F32) + xr0[0 if up else 1, u, d - 1, r, :].astype(F32)).astype(BF16)
            return 0

        lax.fori_loop(0, 8, body, 0)

    group(1, 0)
    go(z_hop(True, 0, 4))
    go(z_hop(False, 1, 4))
    group(1, 1)
    go(z_hop(True, 1, 3))
    go(z_hop(False, 0, 3))
    group(0, 2)
    go(x_hop(True, 0, 2))
    go(x_hop(False, 1, 2))
    z_step(3)
    group(0, 1)
    go(x_hop(True, 1, 1))
    group(0, 3)
    go(x_hop(False, 0, 1))
    x_add(True, 0, 2)
    go(x_hop(True, 0, 1))
    x_add(False, 1, 2)
    go(x_hop(False, 1, 1))
    remote(cvc, cvc, vc_s.at[0], vc_r.at[0], dev_c).wait_recv()
    cv[1] = cv[0] + cvc[...]
    for d in range(1, 4):
        go(remote(cv.at[1], cvx.at[d - 1], vx_s.at[d - 1], vx_r.at[d - 1], dev_x(d)))
    z_step(2)
    group(0, 0)
    for d in range(1, 4):
        remote(cv.at[1], cvx.at[d - 1], vx_s.at[d - 1], vx_r.at[d - 1], dev_x(d)).wait_recv()
    cv[2] = (cv[1] + cvx[0]) + (cvx[1] + cvx[2])
    for d in range(1, 8):
        zz = ((zh * 2 + zl + d) % 8) // 2
        src = cv.at[2, :, pl.ds(pl.multiple_of(zz * BLOCK, BLOCK), BLOCK)]
        go(remote(src, cvz.at[d - 1], vz_s.at[d - 1], vz_r.at[d - 1], dev_z(d)))
    z_step(1)

    def z_copy(d):
        zz = ((zh * 2 + zl + d) % 8) // 2
        return remote(
            s0.at[0, d % 2, pl.ds(pl.multiple_of(zz * BLOCK, BLOCK), BLOCK)], zr0.at[d - 1], z0_s.at[d - 1], z0_r.at[d - 1], dev_z(d)
        )

    for lr, steps in ((1, (1, 7, 3, 5)), (0, (2, 6, 4))):
        x_add(True, lr, 1)
        x_add(False, lr, 1)
        for d in steps:
            go(z_copy(d))

    def x_copy(e):
        return remote(
            s1.at[0, (x + e) % 4, pl.ds(pl.multiple_of(zh * BLOCK, BLOCK), BLOCK)], xr1.at[e - 1], x1_s.at[e - 1], x1_r.at[e - 1], dev_x(e)
        )

    for up in (True, False):
        for u in range(2):
            z_add(up, u, 1)
    for e in range(1, 4):
        go(x_copy(e))

    for d in range(1, 8):
        remote(cvz.at[d - 1], cvz.at[d - 1], vz_s.at[d - 1], vz_r.at[d - 1], dev_z(d)).wait_recv()
    total = cv[2, :, pl.ds(pl.multiple_of(zh * BLOCK, BLOCK), BLOCK)]
    for d in range(7):
        total = total + cvz[d]
    curv[...] = total[:2]

    for d in range(1, 8):
        z_copy(d).wait_recv()
    for e in range(1, 4):
        x_copy(e).wait_recv()

    def last(i, _):
        r = pl.ds(pl.multiple_of(i * 32, 32), 32)
        own = pl.ds(pl.multiple_of(zh * BLOCK + i * 32, 32), 32)
        total = s0[0, 0, own, :].astype(F32)
        for d in range(7):
            total = total + zr0[d, r, :].astype(F32)
        out[0, r, :] = total.astype(BF16)
        total = s1[0, x, own, :].astype(F32)
        for e in range(3):
            total = total + xr1[e, r, :].astype(F32)
        out[1, r, :] = total.astype(BF16)
        return 0

    lax.fori_loop(0, 4, last, 0)
    for up in (True, False):
        for k in range(3):
            block, m = tz_block(up, k)
            tz(up, k, block, m).wait_send()
    for copy in started:
        copy.wait_send()


def on_device(tokens, cotangent, gate_weight, up_weight, down_weight, probe_seeds):
    weights = jnp.concatenate(
        [part.reshape(4, UNITS, COLS) for part in (gate_weight.T, up_weight.T, down_weight)], axis=1
    )
    dma = pltpu.SemaphoreType.DMA
    vmem = pltpu.VMEM
    hbm = pl.BlockSpec(memory_space=pl.ANY)
    tangent, curvature = pl.pallas_call(
        kernel,
        out_shape=(
            jax.ShapeDtypeStruct((2, BLOCK, COLS), BF16),
            jax.ShapeDtypeStruct((2, BLOCK), F32),
        ),
        in_specs=[pl.BlockSpec(memory_space=pltpu.SMEM), hbm, hbm, hbm],
        out_specs=(pl.BlockSpec(memory_space=pltpu.VMEM), pl.BlockSpec(memory_space=pltpu.VMEM)),
        scratch_shapes=[
            vmem((2, 4, 4, 2, 16, D), BF16),
            vmem((4, 4, 3 * UNITS, COLS), BF16),
            vmem((6, UNITS, D), BF16),
            vmem((9, 4 * BLOCK, UNITS), F32),
            vmem((3, 4 * BLOCK, UNITS), BF16),
            vmem((4, 2, 4 * BLOCK, COLS), BF16),
            vmem((4, 2, 4 * BLOCK, COLS), BF16),
            vmem((4, 2, 4 * BLOCK, COLS), BF16),
            vmem((2, 2, 2, 4 * BLOCK, COLS), BF16),
            vmem((7, BLOCK, COLS), BF16),
            vmem((2, 4, 4 * BLOCK, COLS), BF16),
            vmem((2, 4, 4 * BLOCK, COLS), BF16),
            vmem((2, 4, 4 * BLOCK, COLS), BF16),
            vmem((2, 2, 4, 4, 64, COLS), BF16),
            vmem((3, BLOCK, COLS), BF16),
            vmem((3, 8, 4 * BLOCK), F32),
            vmem((8, 4 * BLOCK), F32),
            vmem((3, 8, 4 * BLOCK), F32),
            vmem((7, 8, BLOCK), F32),
            dma((3,)),
            dma((2, 3)), dma((2, 3)),
            dma((2, 4, 3)), dma((2, 4, 3)),
            dma((2, 3)), dma((2, 3)),
            dma((3, 4)), dma((3, 4)),
            dma((3,)), dma((3,)),
            dma((2, 4)), dma((2, 4)),
            dma((2, 2, 2)), dma((2, 2, 2)),
            dma((7,)), dma((7,)),
            dma((2, 2, 4)), dma((2, 2, 4)),
            dma((3,)), dma((3,)),
            dma((1,)), dma((1,)),
            dma((3,)), dma((3,)),
            dma((7,)), dma((7,)),
        ],
        name="curvature_probes",
        cost_estimate=pl.CostEstimate(flops=13 * 2 * 512 * D * UNITS, bytes_accessed=4 * 2**20, transcendentals=512 * UNITS),
        compiler_params=pltpu.CompilerParams(
            collective_id=0, has_side_effects=True, vmem_limit_bytes=60 * 2**20
        ),
    )(
        probe_seeds,
        tokens.reshape(4, 2, 16, D),
        cotangent.reshape(4, 2, 16, D),
        weights,
    )
    return tangent, curvature


def solution(mesh):
    return jax.shard_map(
        on_device,
        mesh=mesh,
        in_specs=(
            P("dp", None),
            P("dp", None),
            P("dp", ("tensor", "probe")),
            P("dp", ("tensor", "probe")),
            P(("tensor", "probe"), "dp"),
            P(),
        ),
        out_specs=(P(None, "dp", ("tensor", "probe")), P(None, "dp")),
        check_vma=False,
    )
```

```python
import functools

import jax
import jax.numpy as jnp
import numpy as np
from jax import lax
from jax.experimental import pallas as pl
from jax.experimental.pallas import tpu as pltpu
from jax.sharding import PartitionSpec as P

D = 4096
FF = 14336
UNITS = 224
COLS = 256
BLOCK = 128
MESH = pl.DeviceIdType.MESH
NT = (((1,), (1,)), ((), ()))
BF16, F32, I32 = jnp.bfloat16, jnp.float32, jnp.int32
IN_FACTOR = float(D**-0.5)
OUT_FACTOR = float(FF**-0.5)
OUT_FACTOR_LOW = float(np.asarray(FF**-0.5, np.float32).astype(jnp.bfloat16))
PARTS = ((0, 2 * UNITS), (2 * UNITS, UNITS))


def wrap(value):
    return np.int32((int(value) + 2**31) % 2**32 - 2**31)


STEP = -1640531535


def kernel(
    seeds, tok, cot, gate, up, down, out, curv,
    wide, wa, tc, w, dirs, acc, hid, cs0, cr0, s0, xr0, zr0, cs1, cr1, s1, zr1, xr1, cv, cvc, cvx, cvz,
    loc_sem, a2a_s, a2a_r, ag_s, ag_r, tz_s, tz_r, tx_s, tx_r, tcc_s, tcc_r,
    c_s, c_r, x0_s, x0_r, z_s, z_r, x1_s, x1_r, vc_s, vc_r, vx_s, vx_r, vz_s, vz_r,
):
    dp, tensor, core = lax.axis_index("dp"), lax.axis_index("tensor"), lax.axis_index("probe")
    zh, y = dp // 4, dp % 4
    zl, x = tensor // 4, tensor % 4

    def dev_z(step):
        z = (zh * 2 + zl + step) % 8
        return ((z // 2) * 4 + y, (z % 2) * 4 + x, core)

    def dev_y(step):
        return (zh * 4 + (y + step) % 4, tensor, core)

    def dev_x(step):
        return (dp, zl * 4 + (x + step) % 4, core)

    dev_c = (dp, tensor, 1 - core)

    def remote(src, dst, send, recv, device):
        return pltpu.make_async_remote_copy(
            src_ref=src, dst_ref=dst, send_sem=send, recv_sem=recv,
            device_id=device, device_id_type=MESH,
        )

    barrier = pltpu.get_barrier_semaphore()
    peers = [dev_z(d) for d in range(1, 8)] + [dev_x(d) for d in range(1, 4)] + [dev_y(1), dev_y(3), dev_c]
    for peer in peers:
        pl.semaphore_signal(barrier, inc=1, device_id=peer, device_id_type=MESH)
    local = [
        pltpu.make_async_copy(tok, tc.at[0, zh], loc_sem.at[0]),
        pltpu.make_async_copy(cot, tc.at[1, zh], loc_sem.at[1]),
        pltpu.make_async_copy(down, wa.at[:, pl.ds(2 * UNITS, UNITS)], loc_sem.at[2]),
        pltpu.make_async_copy(gate, wide.at[0], loc_sem.at[3]),
        pltpu.make_async_copy(up, wide.at[1], loc_sem.at[4]),
    ]
    for k in (3, 4, 2, 0, 1):
        local[k].start()
    for k in range(2):
        local[3 + k].wait()
        wa[:, pl.ds(k * UNITS, UNITS), :] = wide[k].T.reshape(4, UNITS, COLS)
    local[2].wait()
    w[y, zh] = wa[zh]
    pl.semaphore_wait(barrier, len(peers))

    started = []

    def go(copy):
        copy.start()
        started.append(copy)

    def w_at(part, yy, j):
        lo, n = PARTS[part]
        return w.at[yy % 4, (zh + j) % 4, pl.ds(lo, n)]

    def ag_send(part, j):
        lo, n = PARTS[part]
        src = wa.at[zh, pl.ds(lo, n)] if j == 0 else w_at(part, y, j)
        go(remote(src, w_at(part, y, j), ag_s.at[part, j, 0], ag_r.at[part, j, 0], dev_y(1)))
        go(remote(src, w_at(part, y, j), ag_s.at[part, j, 1], ag_r.at[part, j, 1], dev_y(3)))

    def ag_wait(part, j, side, source):
        ref = w_at(part, source, j)
        remote(ref, ref, ag_s.at[part, j, side], ag_r.at[part, j, side], dev_y(1)).wait_recv()

    def ag_relay(part, j):
        side, source, onward = (0, y + 3, 1) if j % 2 == 0 else (1, y + 1, 3)
        ag_wait(part, j, side, source)
        ref = w_at(part, source, j)
        go(remote(ref, ref, ag_s.at[part, j, 2], ag_r.at[part, j, 2], dev_y(onward)))

    def ag_finish(part, j):
        side, source = (1, y + 1) if j % 2 == 0 else (0, y + 3)
        ag_wait(part, j, side, source)
        ag_wait(part, j, 2, y + 2)

    def a2a_send(part, d):
        lo, n = PARTS[part]
        target = (zh + d) % 4
        go(remote(wa.at[target, pl.ds(lo, n)], w_at(part, y, 0), a2a_s.at[part, d - 1], a2a_r.at[part, 3 - d], dev_z(2 * d)))

    def a2a_wait(part, j):
        ref = w_at(part, y, j)
        remote(ref, ref, a2a_s.at[part, j - 1], a2a_r.at[part, j - 1], dev_z(2)).wait_recv()

    HALF = (pl.ds(0, D // 2), pl.ds(D // 2, D // 2))

    def tz(up, k, block, own=False):
        side, m = 0 if up else 1, k % 2
        dst = tc.at[m, block % 4, x, core]
        src = (tok, cot)[m].at[x, core] if own else dst
        if k > 1:
            dst = dst.at[:, HALF[side]]
            src = dst
        return remote(src, dst, tz_s.at[side, k], tz_r.at[side, k], dev_z(1 if up else 7))

    def tz_block(up, k):
        return zh + 2 if k > 1 else zh + 3 if up else zh + 1

    def tz_wait(up, k):
        tz(up, k, tz_block(up, k)).wait_recv()

    def tz_open(k):
        for up in (True, False):

            @pl.when(zl == (1 if up else 0))
            def _():
                tz(up, k, zh, own=True).start()

    def tz_pass(k):
        for up in (True, False):

            @pl.when(zl == (0 if up else 1))
            def _():
                tz_wait(up, k)
                tz(up, k, tz_block(up, k)).start()

    def tz_half(m):
        for up in (True, False):

            @pl.when(zl == (1 if up else 0))
            def _():
                tz_wait(up, m)
                tz(up, m + 2, tz_block(up, m)).start()

    def tz_rest(k):
        for up in (True, False):

            @pl.when(zl == (1 if up else 0))
            def _():
                tz_wait(up, k)

    def tx(j, m, side, source=0):
        ref = tc.at[m, (zh + j) % 4, (x + source) % 4, core]
        return remote(ref, ref, tx_s.at[j - 1, m, side], tx_r.at[j - 1, m, side], dev_x(1 if side == 0 else 3))

    def tx_onward(j, m, side, source):
        ref = tc.at[m, (zh + j) % 4, (x + source) % 4, core, :, HALF[side]]
        return remote(ref, ref, tx_s.at[j - 1, m, 2 + side], tx_r.at[j - 1, m, 2 + side], dev_x(1 if side == 0 else 3))

    def tx_send(m, *js):
        for j in js:
            go(tx(j, m, 0))
            go(tx(j, m, 1))

    def tx_relay(m, *js):
        for j in js:
            for side, source in ((0, 3), (1, 1)):
                tx(j, m, side, source).wait_recv()
                go(tx_onward(j, m, side, source))

    def tok_share(m, *js):
        for j in js:
            for side in range(2):
                tx_onward(j, m, side, 2).wait_recv()
            ref = tc.at[m, (zh + j) % 4, :, core]
            go(remote(ref, ref, tcc_s.at[m, j - 1], tcc_r.at[m, j - 1], dev_c))

    def tok_finish(m):
        for j in (1, 3, 2):
            ref = tc.at[m, (zh + j) % 4, :, 1 - core]
            remote(ref, ref, tcc_s.at[m, j - 1], tcc_r.at[m, j - 1], dev_c).wait_recv()
        local[m].wait()

    first_unit = (tensor * 2 + core) * (4 * UNITS) + zh * UNITS

    def make_signs_of(m, lo, hi):
        unit_mul, feature_mul = (wrap(STEP), wrap(STEP * FF)) if m < 2 else (wrap(STEP * D), wrap(STEP))
        base = (
            lax.broadcasted_iota(I32, (16, D), 0) * unit_mul + lax.broadcasted_iota(I32, (16, D), 1) * feature_mul
        )

        def body(i, _):
            start = (first_unit + i * 16) * unit_mul + np.int32(40503 * (m + 1))
            for p in range(2):
                u = base + (start + seeds[p])
                u = u ^ lax.shift_right_logical(u, np.int32(16))
                u = u * np.int32(739982445)
                u = u ^ lax.shift_right_logical(u, np.int32(13))
                u = u * np.int32(695872825)
                dirs[2 * m + p, pl.ds(pl.multiple_of(i * 16, 16), 16), :] = jnp.where(u < 0, -1.0, 1.0).astype(BF16)
            return 0

        lax.fori_loop(lo, hi, body, 0)

    made = [0]

    def make_signs(n):
        while n:
            m, lo = divmod(made[0], 14)
            take = min(n, 14 - lo)
            make_signs_of(m, lo, lo + take)
            made[0] += take
            n -= take

    def rows_of(m, lo, n):
        return tc[m, pl.ds(lo, n)].reshape(n * BLOCK, D)

    def dir_body(i, _):
        acc[i] = lax.dot_general(rows_of(i // 4, 0, 4), dirs[i], NT, preferred_element_type=F32)
        return 0

    ag_send(0, 0)
    a2a_send(0, 1)
    a2a_send(0, 3)
    tz_open(0)
    tz_open(1)
    ag_send(1, 0)
    make_signs(15)
    ag_relay(0, 0)
    make_signs(14)
    ag_relay(1, 0)
    for j in (1, 3):
        a2a_wait(0, j)
        ag_send(0, j)
    make_signs(3)
    tz_pass(0)
    make_signs(4)
    tz_half(0)
    tx_send(0, 1, 3)
    tz_pass(1)
    make_signs(3)
    tz_pass(2)
    tz_half(1)
    make_signs(3)
    tz_rest(2)
    tx_send(0, 2)
    tz_pass(3)
    a2a_send(0, 2)
    a2a_send(1, 1)
    a2a_send(1, 3)
    a2a_send(1, 2)
    tx_relay(0, 1, 3)
    tx_relay(0, 2)
    tx_send(1, 1, 3)
    tz_rest(3)
    tx_send(1, 2)
    for j in (1, 3):
        ag_relay(0, j)
    tok_share(0, 1, 3, 2)
    tok_finish(0)
    lax.fori_loop(0, 2, dir_body, 0)
    tx_relay(1, 1, 3)
    for j in (2,):
        a2a_wait(0, j)
        ag_send(0, j)
    lax.fori_loop(2, 4, dir_body, 0)
    tx_relay(1, 2)
    ag_relay(0, 2)
    for j in (1, 3, 2):
        a2a_wait(1, j)
        ag_send(1, j)
    tok_share(1, 1, 3, 2)
    tok_finish(1)
    lax.fori_loop(4, 6, dir_body, 0)
    for j in (1, 3):
        ag_relay(1, j)
    for j in (0, 1, 3, 2):
        ag_finish(0, j)

    def plain(i, _):
        rhs = jnp.concatenate([w[b % 4, b // 4, pl.ds(i * UNITS, UNITS), :] for b in range(16)], axis=1)
        acc[6 + i] = lax.dot_general(rows_of(i // 2, 0, 4), rhs, NT, preferred_element_type=F32)
        return 0

    lax.fori_loop(0, 2, plain, 0)
    ag_relay(1, 2)

    def point(i, _):
        r = pl.ds(pl.multiple_of(i * 32, 32), 32)
        gate, up = acc[6, r, :], acc[7, r, :]
        s = jax.nn.sigmoid(gate)
        silu = gate * s
        slope = s * (1.0 + gate * (1.0 - s))
        bend = s * (1.0 - s) * (2.0 + gate * (1.0 - 2.0 * s))
        hid[2, r, :] = (silu * up).astype(BF16)
        for p in range(2):
            gd, ud = acc[p, r, :] * IN_FACTOR, acc[2 + p, r, :] * IN_FACTOR
            hd = slope * gd * up + silu * ud
            hid[p, r, :] = hd.astype(BF16)
            acc[2 + p, r, :] = hd
            acc[p, r, :] = bend * gd * gd * up + 2.0 * slope * gd * ud
        return 0

    lax.fori_loop(0, 16, point, 0)
    for j in (0, 1, 3, 2):
        ag_finish(1, j)

    def curvature_terms():
        cv[0] = jnp.zeros((8, 4 * BLOCK), F32)
        for p in range(2):
            terms = acc[8] * acc[p] + (2.0 * OUT_FACTOR_LOW) * acc[4 + p] * acc[2 + p]
            cv[0, pl.ds(p, 1), :] = jnp.sum(terms.T, axis=0, keepdims=True) * OUT_FACTOR
        go(remote(cv.at[0], cvc, vc_s.at[0], vc_r.at[0], dev_c))

    def columns(e, lr, other):
        return (((zl + lr) % 2) * 4 + (x + e) % 4) * 2 + other

    def tangent(p, b):
        col = pl.ds(pl.multiple_of(b * COLS, COLS), COLS)
        one = jnp.dot(hid[p], w[b % 4, b // 4, pl.ds(2 * UNITS, UNITS), :], preferred_element_type=F32)
        two = jnp.dot(hid[2], dirs[4 + p, :, col], preferred_element_type=F32)
        return one + two * OUT_FACTOR_LOW

    def column(p, g, i, side):
        return columns((i - x) % 4, g, side) if p else columns(g, i, side)

    def give(p, g):
        out_ref, in_ref = (cs1, cr1) if p else (cs0, cr0)
        return remote(out_ref.at[g], in_ref.at[g], c_s.at[p, g], c_r.at[p, g], dev_c)

    def theirs(p, g):
        n, out_ref = (4, cs1) if p else (2, cs0)

        def body(i, _):
            out_ref[g, pl.ds(i, 1)] = tangent(p, column(p, g, i, 1 - core)).astype(BF16)[None]
            return 0

        lax.fori_loop(0, n, body, 0)
        go(give(p, g))

    def ours(p, g):
        n, mine, in_ref = (4, s1, cr1) if p else (2, s0, cr0)
        give(p, g).wait_recv()

        def body(i, _):
            total = tangent(p, column(p, g, i, core)) + in_ref[g, i].astype(F32)
            mine[g, pl.ds(i, 1)] = total.astype(BF16)[None]
            return 0

        lax.fori_loop(0, n, body, 0)

    def z_rows(d, u):
        return pl.ds(pl.multiple_of((((zh * 2 + zl + d) % 8) // 2) * BLOCK + u * 64, 64), 64)

    def z_part(p, up, u, d):
        far = d if up else 8 - d
        rows = z_rows(far, u)
        return s1.at[far % 2, :, rows] if p else s0.at[0, pl.ds(far % 2, 1), rows]

    def z_hop(p, up, u, d):
        side = 0 if up else 1
        land = (zr1 if p else zr0).at[side, u, d - 1]
        return remote(
            z_part(p, up, u, d), land, z_s.at[p, side, u, d - 1], z_r.at[p, side, u, d - 1], dev_z(1 if up else 7)
        )

    def z_add(p, up, u, d):
        z_hop(p, up, u, d).wait_recv()
        far = (d - 1 if up else 9 - d) % 8
        side, r = 0 if up else 1, z_rows(far, u)
        if p:

            def body(i, _):
                s1[far % 2, i, r, :] = (s1[far % 2, i, r, :].astype(F32) + zr1[side, u, d - 1, i].astype(F32)).astype(BF16)
                return 0

            lax.fori_loop(0, 4, body, 0)
        else:
            s0[0, far % 2, r, :] = (s0[0, far % 2, r, :].astype(F32) + zr0[side, u, d - 1, 0].astype(F32)).astype(BF16)

    def z_open(p, d):
        go(z_hop(p, True, 4 - d, d))
        go(z_hop(p, False, d - 3, d))

    def z_lead(p, d):
        for up in (True, False):
            lane = 0 if up else 1
            z_add(p, up, lane, d + 1)
            go(z_hop(p, up, lane, d))

    def z_lag(p, d):
        for up in (True, False):
            lane = 1 if up else 0
            z_add(p, up, lane, d + 1)
            go(z_hop(p, up, lane, d))

    def z_end(p):
        for up in (True, False):
            for u in range(2):
                z_add(p, up, u, 1)

    def x_hop(up, u, d):
        side = 0 if up else 1
        e = d if up else 4 - d
        return remote(s0.at[e, u], xr0.at[side, u, d - 1], x0_s.at[side, u, d - 1], x0_r.at[side, u, d - 1], dev_x(1 if up else 3))

    def x_add(up, u, d):
        x_hop(up, u, d).wait_recv()
        e = (d - 1 if up else 5 - d) % 4

        def body(i, _):
            r = pl.ds(pl.multiple_of(i * 64, 64), 64)
            s0[e, u, r, :] = (s0[e, u, r, :].astype(F32) + xr0[0 if up else 1, u, d - 1, r, :].astype(F32)).astype(BF16)
            return 0

        lax.fori_loop(0, 8, body, 0)

    theirs(0, 2)
    theirs(1, 0)
    ours(0, 2)
    go(x_hop(True, 0, 2))
    go(x_hop(False, 1, 2))
    theirs(1, 1)
    ours(1, 0)
    z_open(1, 4)
    theirs(0, 1)
    ours(1, 1)
    z_open(1, 3)
    theirs(0, 3)
    ours(0, 1)
    go(x_hop(True, 1, 1))
    ours(0, 3)
    go(x_hop(False, 0, 1))
    x_add(True, 0, 2)
    go(x_hop(True, 0, 1))
    x_add(False, 1, 2)
    go(x_hop(False, 1, 1))
    theirs(0, 0)
    z_lead(1, 3)
    ours(0, 0)
    z_lag(1, 2)
    lax.fori_loop(2, 3, plain, 0)
    z_lead(1, 2)
    z_lag(1, 1)
    curvature_terms()
    z_lead(1, 1)
    for lr in range(2):
        x_add(True, lr, 1)
        x_add(False, lr, 1)
    z_open(0, 4)
    z_open(0, 3)
    remote(cvc, cvc, vc_s.at[0], vc_r.at[0], dev_c).wait_recv()
    cv[1] = cv[0] + cvc[...]
    for d in range(1, 4):
        go(remote(cv.at[1], cvx.at[d - 1], vx_s.at[d - 1], vx_r.at[d - 1], dev_x(d)))
    z_end(1)
    z_lead(0, 3)

    def x_copy(e):
        return remote(
            s1.at[0, (x + e) % 4, pl.ds(pl.multiple_of(zh * BLOCK, BLOCK), BLOCK)], xr1.at[e - 1], x1_s.at[e - 1], x1_r.at[e - 1], dev_x(e)
        )

    for e in range(1, 4):
        go(x_copy(e))
    z_lag(0, 2)
    z_lead(0, 2)
    for d in range(1, 4):
        remote(cv.at[1], cvx.at[d - 1], vx_s.at[d - 1], vx_r.at[d - 1], dev_x(d)).wait_recv()
    cv[2] = (cv[1] + cvx[0]) + (cvx[1] + cvx[2])
    for d in range(1, 8):
        zz = ((zh * 2 + zl + d) % 8) // 2
        src = cv.at[2, :, pl.ds(pl.multiple_of(zz * BLOCK, BLOCK), BLOCK)]
        go(remote(src, cvz.at[d - 1], vz_s.at[d - 1], vz_r.at[d - 1], dev_z(d)))
    z_lag(0, 1)
    z_lead(0, 1)

    for d in range(1, 8):
        remote(cvz.at[d - 1], cvz.at[d - 1], vz_s.at[d - 1], vz_r.at[d - 1], dev_z(d)).wait_recv()
    total = cv[2, :, pl.ds(pl.multiple_of(zh * BLOCK, BLOCK), BLOCK)]
    for d in range(7):
        total = total + cvz[d]
    curv[...] = total[:2]

    z_end(0)
    for e in range(1, 4):
        x_copy(e).wait_recv()

    def last(i, _):
        r = pl.ds(pl.multiple_of(i * 32, 32), 32)
        own = pl.ds(pl.multiple_of(zh * BLOCK + i * 32, 32), 32)
        out[0, r, :] = s0[0, 0, own, :]
        total = s1[0, x, own, :].astype(F32)
        for e in range(3):
            total = total + xr1[e, r, :].astype(F32)
        out[1, r, :] = total.astype(BF16)
        return 0

    lax.fori_loop(0, 4, last, 0)
    for up in (True, False):
        for k in range(4):
            tz(up, k, tz_block(up, k)).wait_send()
    for copy in started:
        copy.wait_send()


def on_device(tokens, cotangent, gate_weight, up_weight, down_weight, probe_seeds):
    dma = pltpu.SemaphoreType.DMA
    vmem = pltpu.VMEM
    hbm = pl.BlockSpec(memory_space=pl.ANY)
    tangent, curvature = pl.pallas_call(
        kernel,
        out_shape=(
            jax.ShapeDtypeStruct((2, BLOCK, COLS), BF16),
            jax.ShapeDtypeStruct((2, BLOCK), F32),
        ),
        in_specs=[pl.BlockSpec(memory_space=pltpu.SMEM), hbm, hbm, hbm, hbm, hbm],
        out_specs=(pl.BlockSpec(memory_space=pltpu.VMEM), pl.BlockSpec(memory_space=pltpu.VMEM)),
        scratch_shapes=[
            vmem((2, COLS, 4 * UNITS), BF16),
            vmem((4, 3 * UNITS, COLS), BF16),
            vmem((2, 4, 4, 2, 16, D), BF16),
            vmem((4, 4, 3 * UNITS, COLS), BF16),
            vmem((6, UNITS, D), BF16),
            vmem((9, 4 * BLOCK, UNITS), F32),
            vmem((3, 4 * BLOCK, UNITS), BF16),
            vmem((4, 2, 4 * BLOCK, COLS), BF16),
            vmem((4, 2, 4 * BLOCK, COLS), BF16),
            vmem((4, 2, 4 * BLOCK, COLS), BF16),
            vmem((2, 2, 2, 4 * BLOCK, COLS), BF16),
            vmem((2, 2, 4, 1, 64, COLS), BF16),
            vmem((2, 4, 4 * BLOCK, COLS), BF16),
            vmem((2, 4, 4 * BLOCK, COLS), BF16),
            vmem((2, 4, 4 * BLOCK, COLS), BF16),
            vmem((2, 2, 4, 4, 64, COLS), BF16),
            vmem((3, BLOCK, COLS), BF16),
            vmem((3, 8, 4 * BLOCK), F32),
            vmem((8, 4 * BLOCK), F32),
            vmem((3, 8, 4 * BLOCK), F32),
            vmem((7, 8, BLOCK), F32),
            dma((5,)),
            dma((2, 3)), dma((2, 3)),
            dma((2, 4, 3)), dma((2, 4, 3)),
            dma((2, 4)), dma((2, 4)),
            dma((3, 2, 4)), dma((3, 2, 4)),
            dma((2, 3)), dma((2, 3)),
            dma((2, 4)), dma((2, 4)),
            dma((2, 2, 2)), dma((2, 2, 2)),
            dma((2, 2, 2, 4)), dma((2, 2, 2, 4)),
            dma((3,)), dma((3,)),
            dma((1,)), dma((1,)),
            dma((3,)), dma((3,)),
            dma((7,)), dma((7,)),
        ],
        name="curvature_probes",
        cost_estimate=pl.CostEstimate(flops=13 * 2 * 512 * D * UNITS, bytes_accessed=4 * 2**20, transcendentals=512 * UNITS),
        compiler_params=pltpu.CompilerParams(
            collective_id=0, has_side_effects=True, vmem_limit_bytes=60 * 2**20
        ),
    )(
        probe_seeds,
        tokens.reshape(4, 2, 16, D),
        cotangent.reshape(4, 2, 16, D),
        gate_weight,
        up_weight,
        down_weight.reshape(4, UNITS, COLS),
    )
    return tangent, curvature


def solution(mesh):
    return jax.shard_map(
        on_device,
        mesh=mesh,
        in_specs=(
            P("dp", None),
            P("dp", None),
            P("dp", ("tensor", "probe")),
            P("dp", ("tensor", "probe")),
            P(("tensor", "probe"), "dp"),
            P(),
        ),
        out_specs=(P(None, "dp", ("tensor", "probe")), P(None, "dp")),
        check_vma=False,
    )
```

```python
import functools

import jax
import jax.numpy as jnp
import numpy as np
from jax import lax
from jax.experimental import pallas as pl
from jax.experimental.pallas import tpu as pltpu
from jax.sharding import PartitionSpec as P

D = 4096
FF = 14336
UNITS = 224
COLS = 256
BLOCK = 128
MESH = pl.DeviceIdType.MESH
NT = (((1,), (1,)), ((), ()))
BF16, F32, I32 = jnp.bfloat16, jnp.float32, jnp.int32
IN_FACTOR = float(D**-0.5)
OUT_FACTOR = float(FF**-0.5)
OUT_FACTOR_LOW = float(np.asarray(FF**-0.5, np.float32).astype(jnp.bfloat16))
PARTS = ((0, 2 * UNITS), (2 * UNITS, UNITS))


def wrap(value):
    return np.int32((int(value) + 2**31) % 2**32 - 2**31)


STEP = -1640531535


def kernel(
    seeds, tok, cot, gate, up, down, out, curv,
    wide, wa, tc, w, dirs, acc, hid, cs0, cr0, s0, xr0, zr0, cs1, cr1, s1, zr1, xr1, cv, cvc, cvx, cvz,
    loc_sem, a2a_s, a2a_r, ag_s, ag_r, tz_s, tz_r, tx_s, tx_r, tcc_s, tcc_r,
    c_s, c_r, x0_s, x0_r, z_s, z_r, x1_s, x1_r, vc_s, vc_r, vx_s, vx_r, vz_s, vz_r,
):
    dp, tensor, core = lax.axis_index("dp"), lax.axis_index("tensor"), lax.axis_index("probe")
    zh, y = dp // 4, dp % 4
    zl, x = tensor // 4, tensor % 4

    def dev_z(step):
        z = (zh * 2 + zl + step) % 8
        return ((z // 2) * 4 + y, (z % 2) * 4 + x, core)

    def dev_y(step):
        return (zh * 4 + (y + step) % 4, tensor, core)

    def dev_x(step):
        return (dp, zl * 4 + (x + step) % 4, core)

    dev_c = (dp, tensor, 1 - core)

    def remote(src, dst, send, recv, device):
        return pltpu.make_async_remote_copy(
            src_ref=src, dst_ref=dst, send_sem=send, recv_sem=recv,
            device_id=device, device_id_type=MESH,
        )

    barrier = pltpu.get_barrier_semaphore()
    peers = [dev_z(d) for d in range(1, 8)] + [dev_x(d) for d in range(1, 4)] + [dev_y(1), dev_y(3), dev_c]
    for peer in peers:
        pl.semaphore_signal(barrier, inc=1, device_id=peer, device_id_type=MESH)
    local = [
        pltpu.make_async_copy(tok, tc.at[0, zh], loc_sem.at[0]),
        pltpu.make_async_copy(cot, tc.at[1, zh], loc_sem.at[1]),
        pltpu.make_async_copy(down, wa.at[:, pl.ds(2 * UNITS, UNITS)], loc_sem.at[2]),
        pltpu.make_async_copy(gate, wide.at[0], loc_sem.at[3]),
        pltpu.make_async_copy(up, wide.at[1], loc_sem.at[4]),
    ]
    for k in (3, 4, 2, 0, 1):
        local[k].start()
    for k in range(2):
        local[3 + k].wait()
        wa[:, pl.ds(k * UNITS, UNITS), :] = wide[k].T.reshape(4, UNITS, COLS)
    local[2].wait()
    w[y, zh] = wa[zh]
    pl.semaphore_wait(barrier, len(peers))

    started = []

    def go(copy):
        copy.start()
        started.append(copy)

    def w_at(part, yy, j):
        lo, n = PARTS[part]
        return w.at[yy % 4, (zh + j) % 4, pl.ds(lo, n)]

    def ag_send(part, j):
        lo, n = PARTS[part]
        src = wa.at[zh, pl.ds(lo, n)] if j == 0 else w_at(part, y, j)
        go(remote(src, w_at(part, y, j), ag_s.at[part, j, 0], ag_r.at[part, j, 0], dev_y(1)))
        go(remote(src, w_at(part, y, j), ag_s.at[part, j, 1], ag_r.at[part, j, 1], dev_y(3)))

    def ag_wait(part, j, side, source):
        ref = w_at(part, source, j)
        remote(ref, ref, ag_s.at[part, j, side], ag_r.at[part, j, side], dev_y(1)).wait_recv()

    def ag_relay(part, j):
        side, source, onward = (0, y + 3, 1) if j % 2 == 0 else (1, y + 1, 3)
        ag_wait(part, j, side, source)
        ref = w_at(part, source, j)
        go(remote(ref, ref, ag_s.at[part, j, 2], ag_r.at[part, j, 2], dev_y(onward)))

    def ag_finish(part, j):
        side, source = (1, y + 1) if j % 2 == 0 else (0, y + 3)
        ag_wait(part, j, side, source)
        ag_wait(part, j, 2, y + 2)

    def a2a_send(part, d):
        lo, n = PARTS[part]
        target = (zh + d) % 4
        go(remote(wa.at[target, pl.ds(lo, n)], w_at(part, y, 0), a2a_s.at[part, d - 1], a2a_r.at[part, 3 - d], dev_z(2 * d)))

    def a2a_wait(part, j):
        ref = w_at(part, y, j)
        remote(ref, ref, a2a_s.at[part, j - 1], a2a_r.at[part, j - 1], dev_z(2)).wait_recv()

    HALF = (pl.ds(0, D // 2), pl.ds(D // 2, D // 2))

    def tz(up, k, block, own=False):
        side, m = 0 if up else 1, k % 2
        dst = tc.at[m, block % 4, x, core]
        src = (tok, cot)[m].at[x, core] if own else dst
        if k > 1:
            dst = dst.at[:, HALF[side]]
            src = dst
        return remote(src, dst, tz_s.at[side, k], tz_r.at[side, k], dev_z(1 if up else 7))

    def tz_block(up, k):
        return zh + 2 if k > 1 else zh + 3 if up else zh + 1

    def tz_wait(up, k):
        tz(up, k, tz_block(up, k)).wait_recv()

    def tz_open(k):
        for up in (True, False):

            @pl.when(zl == (1 if up else 0))
            def _():
                tz(up, k, zh, own=True).start()

    def tz_pass(k):
        for up in (True, False):

            @pl.when(zl == (0 if up else 1))
            def _():
                tz_wait(up, k)
                tz(up, k, tz_block(up, k)).start()

    def tz_half(m):
        for up in (True, False):

            @pl.when(zl == (1 if up else 0))
            def _():
                tz_wait(up, m)
                tz(up, m + 2, tz_block(up, m)).start()

    def tz_rest(k):
        for up in (True, False):

            @pl.when(zl == (1 if up else 0))
            def _():
                tz_wait(up, k)

    def tx(j, m, side, source=0):
        ref = tc.at[m, (zh + j) % 4, (x + source) % 4, core]
        return remote(ref, ref, tx_s.at[j - 1, m, side], tx_r.at[j - 1, m, side], dev_x(1 if side == 0 else 3))

    def tx_onward(j, m, side, source):
        ref = tc.at[m, (zh + j) % 4, (x + source) % 4, core, :, HALF[side]]
        return remote(ref, ref, tx_s.at[j - 1, m, 2 + side], tx_r.at[j - 1, m, 2 + side], dev_x(1 if side == 0 else 3))

    def tx_send(m, *js):
        for j in js:
            go(tx(j, m, 0))
            go(tx(j, m, 1))

    def tx_relay(m, *js):
        for j in js:
            for side, source in ((0, 3), (1, 1)):
                tx(j, m, side, source).wait_recv()
                go(tx_onward(j, m, side, source))

    def tok_share(m, *js):
        for j in js:
            for side in range(2):
                tx_onward(j, m, side, 2).wait_recv()
            ref = tc.at[m, (zh + j) % 4, :, core]
            go(remote(ref, ref, tcc_s.at[m, j - 1], tcc_r.at[m, j - 1], dev_c))

    def tok_finish(m):
        for j in (1, 3, 2):
            ref = tc.at[m, (zh + j) % 4, :, 1 - core]
            remote(ref, ref, tcc_s.at[m, j - 1], tcc_r.at[m, j - 1], dev_c).wait_recv()
        local[m].wait()

    first_unit = (tensor * 2 + core) * (4 * UNITS) + zh * UNITS

    def make_signs_of(m, lo, hi):
        unit_mul, feature_mul = (wrap(STEP), wrap(STEP * FF)) if m < 2 else (wrap(STEP * D), wrap(STEP))
        base = (
            lax.broadcasted_iota(I32, (16, D), 0) * unit_mul + lax.broadcasted_iota(I32, (16, D), 1) * feature_mul
        )

        def body(i, _):
            start = (first_unit + i * 16) * unit_mul + np.int32(40503 * (m + 1))
            for p in range(2):
                u = base + (start + seeds[p])
                u = u ^ lax.shift_right_logical(u, np.int32(16))
                u = u * np.int32(739982445)
                u = u ^ lax.shift_right_logical(u, np.int32(13))
                u = u * np.int32(695872825)
                dirs[2 * m + p, pl.ds(pl.multiple_of(i * 16, 16), 16), :] = jnp.where(u < 0, -1.0, 1.0).astype(BF16)
            return 0

        lax.fori_loop(lo, hi, body, 0)

    made = [0]

    def make_signs(n):
        while n:
            m, lo = divmod(made[0], 14)
            take = min(n, 14 - lo)
            make_signs_of(m, lo, lo + take)
            made[0] += take
            n -= take

    def rows_of(m, lo, n):
        return tc[m, pl.ds(lo, n)].reshape(n * BLOCK, D)

    def dir_body(i, _):
        acc[i] = lax.dot_general(rows_of(i // 4, 0, 4), dirs[i], NT, preferred_element_type=F32)
        return 0

    ag_send(0, 0)
    a2a_send(0, 1)
    a2a_send(0, 3)
    a2a_send(0, 2)
    tz_open(0)
    tz_open(1)
    ag_send(1, 0)
    make_signs(15)
    ag_relay(0, 0)
    make_signs(6)
    for j in (1, 3):
        a2a_wait(0, j)
        ag_send(0, j)
    tz_pass(0)
    tz_pass(1)
    ag_relay(1, 0)
    make_signs(9)
    tz_half(0)
    tx_send(0, 1, 3)
    tz_half(1)
    a2a_wait(0, 2)
    ag_send(0, 2)
    make_signs(6)
    for j in (1, 3):
        ag_relay(0, j)
    tz_pass(2)
    tz_pass(3)
    for d in (1, 3, 2):
        a2a_send(1, d)
    make_signs(6)
    tz_rest(2)
    tx_send(0, 2)
    tx_relay(0, 1, 3)
    tx_relay(0, 2)
    tx_send(1, 1, 3)
    ag_relay(0, 2)
    tok_share(0, 1, 3, 2)
    tz_rest(3)
    tx_send(1, 2)
    tok_finish(0)
    lax.fori_loop(0, 1, dir_body, 0)
    for j in (1, 3):
        a2a_wait(1, j)
        ag_send(1, j)
    tx_relay(1, 1, 3)
    lax.fori_loop(1, 3, dir_body, 0)
    a2a_wait(1, 2)
    ag_send(1, 2)
    tx_relay(1, 2)
    lax.fori_loop(3, 4, dir_body, 0)
    for j in (0, 1, 3, 2):
        ag_finish(0, j)

    def plain(i, _):
        rhs = jnp.concatenate([w[b % 4, b // 4, pl.ds(i * UNITS, UNITS), :] for b in range(16)], axis=1)
        acc[6 + i] = lax.dot_general(rows_of(i // 2, 0, 4), rhs, NT, preferred_element_type=F32)
        return 0

    lax.fori_loop(0, 2, plain, 0)
    for j in (1, 3):
        ag_relay(1, j)
    tok_share(1, 1, 3, 2)

    def point(i, _):
        r = pl.ds(pl.multiple_of(i * 32, 32), 32)
        gate, up = acc[6, r, :], acc[7, r, :]
        s = jax.nn.sigmoid(gate)
        silu = gate * s
        slope = s * (1.0 + gate * (1.0 - s))
        bend = s * (1.0 - s) * (2.0 + gate * (1.0 - 2.0 * s))
        hid[2, r, :] = (silu * up).astype(BF16)
        for p in range(2):
            gd, ud = acc[p, r, :] * IN_FACTOR, acc[2 + p, r, :] * IN_FACTOR
            hd = slope * gd * up + silu * ud
            hid[p, r, :] = hd.astype(BF16)
            acc[2 + p, r, :] = hd
            acc[p, r, :] = bend * gd * gd * up + 2.0 * slope * gd * ud
        return 0

    lax.fori_loop(0, 16, point, 0)
    ag_relay(1, 2)
    tok_finish(1)
    lax.fori_loop(4, 6, dir_body, 0)
    for j in (0, 1, 3, 2):
        ag_finish(1, j)

    def curvature_terms():
        cv[0] = jnp.zeros((8, 4 * BLOCK), F32)
        for p in range(2):
            terms = acc[8] * acc[p] + (2.0 * OUT_FACTOR_LOW) * acc[4 + p] * acc[2 + p]
            cv[0, pl.ds(p, 1), :] = jnp.sum(terms.T, axis=0, keepdims=True) * OUT_FACTOR
        go(remote(cv.at[0], cvc, vc_s.at[0], vc_r.at[0], dev_c))

    def columns(e, lr, other):
        return (((zl + lr) % 2) * 4 + (x + e) % 4) * 2 + other

    def tangent(p, b):
        col = pl.ds(pl.multiple_of(b * COLS, COLS), COLS)
        one = jnp.dot(hid[p], w[b % 4, b // 4, pl.ds(2 * UNITS, UNITS), :], preferred_element_type=F32)
        two = jnp.dot(hid[2], dirs[4 + p, :, col], preferred_element_type=F32)
        return one + two * OUT_FACTOR_LOW

    def column(p, g, i, side):
        return columns((i - x) % 4, g, side) if p else columns(g, i, side)

    def give(p, g):
        out_ref, in_ref = (cs1, cr1) if p else (cs0, cr0)
        return remote(out_ref.at[g], in_ref.at[g], c_s.at[p, g], c_r.at[p, g], dev_c)

    def theirs(p, g):
        n, out_ref = (4, cs1) if p else (2, cs0)

        def body(i, _):
            out_ref[g, pl.ds(i, 1)] = tangent(p, column(p, g, i, 1 - core)).astype(BF16)[None]
            return 0

        lax.fori_loop(0, n, body, 0)
        go(give(p, g))

    def ours(p, g):
        n, mine, in_ref = (4, s1, cr1) if p else (2, s0, cr0)
        give(p, g).wait_recv()

        def body(i, _):
            total = tangent(p, column(p, g, i, core)) + in_ref[g, i].astype(F32)
            mine[g, pl.ds(i, 1)] = total.astype(BF16)[None]
            return 0

        lax.fori_loop(0, n, body, 0)

    def z_rows(d, u):
        return pl.ds(pl.multiple_of((((zh * 2 + zl + d) % 8) // 2) * BLOCK + u * 64, 64), 64)

    def z_part(p, up, u, d):
        far = d if up else 8 - d
        rows = z_rows(far, u)
        return s1.at[far % 2, :, rows] if p else s0.at[0, pl.ds(far % 2, 1), rows]

    def z_hop(p, up, u, d):
        side = 0 if up else 1
        land = (zr1 if p else zr0).at[side, u, d - 1]
        return remote(
            z_part(p, up, u, d), land, z_s.at[p, side, u, d - 1], z_r.at[p, side, u, d - 1], dev_z(1 if up else 7)
        )

    def z_add(p, up, u, d):
        z_hop(p, up, u, d).wait_recv()
        far = (d - 1 if up else 9 - d) % 8
        side, r = 0 if up else 1, z_rows(far, u)
        if p:

            def body(i, _):
                s1[far % 2, i, r, :] = (s1[far % 2, i, r, :].astype(F32) + zr1[side, u, d - 1, i].astype(F32)).astype(BF16)
                return 0

            lax.fori_loop(0, 4, body, 0)
        else:
            s0[0, far % 2, r, :] = (s0[0, far % 2, r, :].astype(F32) + zr0[side, u, d - 1, 0].astype(F32)).astype(BF16)

    def z_open(p, d):
        go(z_hop(p, True, 4 - d, d))
        go(z_hop(p, False, d - 3, d))

    def z_lead(p, d):
        for up in (True, False):
            lane = 0 if up else 1
            z_add(p, up, lane, d + 1)
            go(z_hop(p, up, lane, d))

    def z_lag(p, d):
        for up in (True, False):
            lane = 1 if up else 0
            z_add(p, up, lane, d + 1)
            go(z_hop(p, up, lane, d))

    def z_end(p):
        for up in (True, False):
            for u in range(2):
                z_add(p, up, u, 1)

    def x_hop(up, u, d):
        side = 0 if up else 1
        e = d if up else 4 - d
        return remote(s0.at[e, u], xr0.at[side, u, d - 1], x0_s.at[side, u, d - 1], x0_r.at[side, u, d - 1], dev_x(1 if up else 3))

    def x_add(up, u, d):
        x_hop(up, u, d).wait_recv()
        e = (d - 1 if up else 5 - d) % 4

        def body(i, _):
            r = pl.ds(pl.multiple_of(i * 64, 64), 64)
            s0[e, u, r, :] = (s0[e, u, r, :].astype(F32) + xr0[0 if up else 1, u, d - 1, r, :].astype(F32)).astype(BF16)
            return 0

        lax.fori_loop(0, 8, body, 0)

    theirs(0, 2)
    theirs(1, 0)
    ours(0, 2)
    go(x_hop(True, 0, 2))
    go(x_hop(False, 1, 2))
    theirs(1, 1)
    ours(1, 0)
    z_open(1, 4)
    theirs(0, 1)
    ours(1, 1)
    z_open(1, 3)
    theirs(0, 3)
    ours(0, 1)
    go(x_hop(True, 1, 1))
    ours(0, 3)
    go(x_hop(False, 0, 1))
    x_add(True, 0, 2)
    go(x_hop(True, 0, 1))
    x_add(False, 1, 2)
    go(x_hop(False, 1, 1))
    theirs(0, 0)
    z_lead(1, 3)
    ours(0, 0)
    z_lag(1, 2)
    lax.fori_loop(2, 3, plain, 0)
    z_lead(1, 2)
    z_lag(1, 1)
    curvature_terms()
    z_lead(1, 1)
    for lr in range(2):
        x_add(True, lr, 1)
        x_add(False, lr, 1)
    z_open(0, 4)
    z_open(0, 3)
    remote(cvc, cvc, vc_s.at[0], vc_r.at[0], dev_c).wait_recv()
    cv[1] = cv[0] + cvc[...]
    for d in range(1, 4):
        go(remote(cv.at[1], cvx.at[d - 1], vx_s.at[d - 1], vx_r.at[d - 1], dev_x(d)))
    z_end(1)
    z_lead(0, 3)

    def x_copy(e):
        return remote(
            s1.at[0, (x + e) % 4, pl.ds(pl.multiple_of(zh * BLOCK, BLOCK), BLOCK)], xr1.at[e - 1], x1_s.at[e - 1], x1_r.at[e - 1], dev_x(e)
        )

    for e in range(1, 4):
        go(x_copy(e))
    z_lag(0, 2)
    z_lead(0, 2)
    for d in range(1, 4):
        remote(cv.at[1], cvx.at[d - 1], vx_s.at[d - 1], vx_r.at[d - 1], dev_x(d)).wait_recv()
    cv[2] = (cv[1] + cvx[0]) + (cvx[1] + cvx[2])
    for d in range(1, 8):
        zz = ((zh * 2 + zl + d) % 8) // 2
        src = cv.at[2, :, pl.ds(pl.multiple_of(zz * BLOCK, BLOCK), BLOCK)]
        go(remote(src, cvz.at[d - 1], vz_s.at[d - 1], vz_r.at[d - 1], dev_z(d)))
    z_lag(0, 1)
    z_lead(0, 1)

    for d in range(1, 8):
        remote(cvz.at[d - 1], cvz.at[d - 1], vz_s.at[d - 1], vz_r.at[d - 1], dev_z(d)).wait_recv()
    total = cv[2, :, pl.ds(pl.multiple_of(zh * BLOCK, BLOCK), BLOCK)]
    for d in range(7):
        total = total + cvz[d]
    curv[...] = total[:2]

    z_end(0)
    for e in range(1, 4):
        x_copy(e).wait_recv()

    def last(i, _):
        r = pl.ds(pl.multiple_of(i * 32, 32), 32)
        own = pl.ds(pl.multiple_of(zh * BLOCK + i * 32, 32), 32)
        out[0, r, :] = s0[0, 0, own, :]
        total = s1[0, x, own, :].astype(F32)
        for e in range(3):
            total = total + xr1[e, r, :].astype(F32)
        out[1, r, :] = total.astype(BF16)
        return 0

    lax.fori_loop(0, 4, last, 0)
    for up in (True, False):
        for k in range(4):
            tz(up, k, tz_block(up, k)).wait_send()
    for copy in started:
        copy.wait_send()


def on_device(tokens, cotangent, gate_weight, up_weight, down_weight, probe_seeds):
    dma = pltpu.SemaphoreType.DMA
    vmem = pltpu.VMEM
    hbm = pl.BlockSpec(memory_space=pl.ANY)
    tangent, curvature = pl.pallas_call(
        kernel,
        out_shape=(
            jax.ShapeDtypeStruct((2, BLOCK, COLS), BF16),
            jax.ShapeDtypeStruct((2, BLOCK), F32),
        ),
        in_specs=[pl.BlockSpec(memory_space=pltpu.SMEM), hbm, hbm, hbm, hbm, hbm],
        out_specs=(pl.BlockSpec(memory_space=pltpu.VMEM), pl.BlockSpec(memory_space=pltpu.VMEM)),
        scratch_shapes=[
            vmem((2, COLS, 4 * UNITS), BF16),
            vmem((4, 3 * UNITS, COLS), BF16),
            vmem((2, 4, 4, 2, 16, D), BF16),
            vmem((4, 4, 3 * UNITS, COLS), BF16),
            vmem((6, UNITS, D), BF16),
            vmem((9, 4 * BLOCK, UNITS), F32),
            vmem((3, 4 * BLOCK, UNITS), BF16),
            vmem((4, 2, 4 * BLOCK, COLS), BF16),
            vmem((4, 2, 4 * BLOCK, COLS), BF16),
            vmem((4, 2, 4 * BLOCK, COLS), BF16),
            vmem((2, 2, 2, 4 * BLOCK, COLS), BF16),
            vmem((2, 2, 4, 1, 64, COLS), BF16),
            vmem((2, 4, 4 * BLOCK, COLS), BF16),
            vmem((2, 4, 4 * BLOCK, COLS), BF16),
            vmem((2, 4, 4 * BLOCK, COLS), BF16),
            vmem((2, 2, 4, 4, 64, COLS), BF16),
            vmem((3, BLOCK, COLS), BF16),
            vmem((3, 8, 4 * BLOCK), F32),
            vmem((8, 4 * BLOCK), F32),
            vmem((3, 8, 4 * BLOCK), F32),
            vmem((7, 8, BLOCK), F32),
            dma((5,)),
            dma((2, 3)), dma((2, 3)),
            dma((2, 4, 3)), dma((2, 4, 3)),
            dma((2, 4)), dma((2, 4)),
            dma((3, 2, 4)), dma((3, 2, 4)),
            dma((2, 3)), dma((2, 3)),
            dma((2, 4)), dma((2, 4)),
            dma((2, 2, 2)), dma((2, 2, 2)),
            dma((2, 2, 2, 4)), dma((2, 2, 2, 4)),
            dma((3,)), dma((3,)),
            dma((1,)), dma((1,)),
            dma((3,)), dma((3,)),
            dma((7,)), dma((7,)),
        ],
        name="curvature_probes",
        cost_estimate=pl.CostEstimate(flops=13 * 2 * 512 * D * UNITS, bytes_accessed=4 * 2**20, transcendentals=512 * UNITS),
        compiler_params=pltpu.CompilerParams(
            collective_id=0, has_side_effects=True, vmem_limit_bytes=60 * 2**20
        ),
    )(
        probe_seeds,
        tokens.reshape(4, 2, 16, D),
        cotangent.reshape(4, 2, 16, D),
        gate_weight,
        up_weight,
        down_weight.reshape(4, UNITS, COLS),
    )
    return tangent, curvature


def solution(mesh):
    return jax.shard_map(
        on_device,
        mesh=mesh,
        in_specs=(
            P("dp", None),
            P("dp", None),
            P("dp", ("tensor", "probe")),
            P("dp", ("tensor", "probe")),
            P(("tensor", "probe"), "dp"),
            P(),
        ),
        out_specs=(P(None, "dp", ("tensor", "probe")), P(None, "dp")),
        check_vma=False,
    )
```

```python
import functools

import jax
import jax.numpy as jnp
import numpy as np
from jax import lax
from jax.experimental import pallas as pl
from jax.experimental.pallas import tpu as pltpu
from jax.sharding import PartitionSpec as P

D = 4096
FF = 14336
UNITS = 224
COLS = 256
BLOCK = 128
MESH = pl.DeviceIdType.MESH
NT = (((1,), (1,)), ((), ()))
BF16, F32, I32 = jnp.bfloat16, jnp.float32, jnp.int32
IN_FACTOR = float(D**-0.5)
OUT_FACTOR = float(FF**-0.5)
OUT_FACTOR_LOW = float(np.asarray(FF**-0.5, np.float32).astype(jnp.bfloat16))
PARTS = ((0, 2 * UNITS), (2 * UNITS, UNITS))


def wrap(value):
    return np.int32((int(value) + 2**31) % 2**32 - 2**31)


STEP = -1640531535


def kernel(
    seeds, tok, cot, gate, up, down, out, curv,
    wide, wa, tc, w, dirs, acc, hid, cs0, cr0, s0, xr0, zr0, cs1, cr1, s1, zr1, xr1, cv, cvc, cvx, cvz,
    loc_sem, a2a_s, a2a_r, ag_s, ag_r, tz_s, tz_r, tx_s, tx_r, tcc_s, tcc_r,
    c_s, c_r, x0_s, x0_r, z_s, z_r, x1_s, x1_r, vc_s, vc_r, vx_s, vx_r, vz_s, vz_r,
):
    dp, tensor, core = lax.axis_index("dp"), lax.axis_index("tensor"), lax.axis_index("probe")
    zh, y = dp // 4, dp % 4
    zl, x = tensor // 4, tensor % 4

    def dev_z(step):
        z = (zh * 2 + zl + step) % 8
        return ((z // 2) * 4 + y, (z % 2) * 4 + x, core)

    def dev_y(step):
        return (zh * 4 + (y + step) % 4, tensor, core)

    def dev_x(step):
        return (dp, zl * 4 + (x + step) % 4, core)

    dev_c = (dp, tensor, 1 - core)

    def remote(src, dst, send, recv, device):
        return pltpu.make_async_remote_copy(
            src_ref=src, dst_ref=dst, send_sem=send, recv_sem=recv,
            device_id=device, device_id_type=MESH,
        )

    barrier = pltpu.get_barrier_semaphore()
    peers = [dev_z(d) for d in range(1, 8)] + [dev_x(d) for d in range(1, 4)] + [dev_y(1), dev_y(3), dev_c]
    for peer in peers:
        pl.semaphore_signal(barrier, inc=1, device_id=peer, device_id_type=MESH)
    local = [
        pltpu.make_async_copy(tok, tc.at[0, zh], loc_sem.at[0]),
        pltpu.make_async_copy(cot, tc.at[1, zh], loc_sem.at[1]),
        pltpu.make_async_copy(down, wa.at[:, pl.ds(2 * UNITS, UNITS)], loc_sem.at[2]),
        pltpu.make_async_copy(gate, wide.at[0], loc_sem.at[3]),
        pltpu.make_async_copy(up, wide.at[1], loc_sem.at[4]),
    ]
    for k in (3, 4, 2, 0, 1):
        local[k].start()
    for k in range(2):
        local[3 + k].wait()
        wa[:, pl.ds(k * UNITS, UNITS), :] = wide[k].T.reshape(4, UNITS, COLS)
    local[2].wait()
    w[y, zh] = wa[zh]
    pl.semaphore_wait(barrier, len(peers))

    started = []

    def go(copy):
        copy.start()
        started.append(copy)

    def w_at(part, yy, j):
        lo, n = PARTS[part]
        return w.at[yy % 4, (zh + j) % 4, pl.ds(lo, n)]

    def ag_send(part, j):
        lo, n = PARTS[part]
        src = wa.at[zh, pl.ds(lo, n)] if j == 0 else w_at(part, y, j)
        go(remote(src, w_at(part, y, j), ag_s.at[part, j, 0], ag_r.at[part, j, 0], dev_y(1)))
        go(remote(src, w_at(part, y, j), ag_s.at[part, j, 1], ag_r.at[part, j, 1], dev_y(3)))

    def ag_wait(part, j, side, source):
        ref = w_at(part, source, j)
        remote(ref, ref, ag_s.at[part, j, side], ag_r.at[part, j, side], dev_y(1)).wait_recv()

    def ag_relay(part, j):
        side, source, onward = (0, y + 3, 1) if j % 2 == 0 else (1, y + 1, 3)
        ag_wait(part, j, side, source)
        ref = w_at(part, source, j)
        go(remote(ref, ref, ag_s.at[part, j, 2], ag_r.at[part, j, 2], dev_y(onward)))

    def ag_finish(part, j):
        side, source = (1, y + 1) if j % 2 == 0 else (0, y + 3)
        ag_wait(part, j, side, source)
        ag_wait(part, j, 2, y + 2)

    def a2a_send(part, d):
        lo, n = PARTS[part]
        target = (zh + d) % 4
        go(remote(wa.at[target, pl.ds(lo, n)], w_at(part, y, 0), a2a_s.at[part, d - 1], a2a_r.at[part, 3 - d], dev_z(2 * d)))

    def a2a_far(k):
        rows = pl.ds(k * UNITS, UNITS)
        return remote(
            wa.at[(zh + 2) % 4, rows], w.at[y, zh, rows], a2a_s.at[0, 1 + 2 * k], a2a_r.at[0, 1 + 2 * k], dev_z(4)
        )

    def a2a_far_wait():
        for k in range(2):
            a2a_far(k).wait_recv()

    def a2a_wait(part, j):
        ref = w_at(part, y, j)
        remote(ref, ref, a2a_s.at[part, j - 1], a2a_r.at[part, j - 1], dev_z(2)).wait_recv()

    HALF = (pl.ds(0, D // 2), pl.ds(D // 2, D // 2))

    def tz(up, k, block, own=False):
        side, m = 0 if up else 1, k % 2
        dst = tc.at[m, block % 4, x, core]
        src = (tok, cot)[m].at[x, core] if own else dst
        if k > 1:
            dst = dst.at[:, HALF[side]]
            src = dst
        return remote(src, dst, tz_s.at[side, k], tz_r.at[side, k], dev_z(1 if up else 7))

    def tz_block(up, k):
        return zh + 2 if k > 1 else zh + 3 if up else zh + 1

    def tz_wait(up, k):
        tz(up, k, tz_block(up, k)).wait_recv()

    def tz_open(k):
        for up in (True, False):

            @pl.when(zl == (1 if up else 0))
            def _():
                tz(up, k, zh, own=True).start()

    def tz_pass(k):
        for up in (True, False):

            @pl.when(zl == (0 if up else 1))
            def _():
                tz_wait(up, k)
                tz(up, k, tz_block(up, k)).start()

    def tz_half(m):
        for up in (True, False):

            @pl.when(zl == (1 if up else 0))
            def _():
                tz_wait(up, m)
                tz(up, m + 2, tz_block(up, m)).start()

    def tz_rest(k):
        for up in (True, False):

            @pl.when(zl == (1 if up else 0))
            def _():
                tz_wait(up, k)

    def tx(j, m, side, source=0):
        ref = tc.at[m, (zh + j) % 4, (x + source) % 4, core]
        return remote(ref, ref, tx_s.at[j - 1, m, side], tx_r.at[j - 1, m, side], dev_x(1 if side == 0 else 3))

    def tx_onward(j, m, side, source):
        ref = tc.at[m, (zh + j) % 4, (x + source) % 4, core, :, HALF[side]]
        return remote(ref, ref, tx_s.at[j - 1, m, 2 + side], tx_r.at[j - 1, m, 2 + side], dev_x(1 if side == 0 else 3))

    def tx_send(m, *js):
        for j in js:
            go(tx(j, m, 0))
            go(tx(j, m, 1))

    def tx_relay(m, *js):
        for j in js:
            for side, source in ((0, 3), (1, 1)):
                tx(j, m, side, source).wait_recv()
                go(tx_onward(j, m, side, source))

    def tok_share(m, *js):
        for j in js:
            for side in range(2):
                tx_onward(j, m, side, 2).wait_recv()
            ref = tc.at[m, (zh + j) % 4, :, core]
            go(remote(ref, ref, tcc_s.at[m, j - 1], tcc_r.at[m, j - 1], dev_c))

    def tok_finish(m):
        for j in (1, 3, 2):
            ref = tc.at[m, (zh + j) % 4, :, 1 - core]
            remote(ref, ref, tcc_s.at[m, j - 1], tcc_r.at[m, j - 1], dev_c).wait_recv()
        local[m].wait()

    first_unit = (tensor * 2 + core) * (4 * UNITS) + zh * UNITS

    def make_signs_of(m, lo, hi):
        unit_mul, feature_mul = (wrap(STEP), wrap(STEP * FF)) if m < 2 else (wrap(STEP * D), wrap(STEP))
        base = (
            lax.broadcasted_iota(I32, (16, D), 0) * unit_mul + lax.broadcasted_iota(I32, (16, D), 1) * feature_mul
        )

        def body(i, _):
            start = (first_unit + i * 16) * unit_mul + np.int32(40503 * (m + 1))
            for p in range(2):
                u = base + (start + seeds[p])
                u = u ^ lax.shift_right_logical(u, np.int32(16))
                u = u * np.int32(739982445)
                u = u ^ lax.shift_right_logical(u, np.int32(13))
                u = u * np.int32(695872825)
                dirs[2 * m + p, pl.ds(pl.multiple_of(i * 16, 16), 16), :] = jnp.where(u < 0, -1.0, 1.0).astype(BF16)
            return 0

        lax.fori_loop(lo, hi, body, 0)

    made = [0]

    def make_signs(n):
        while n:
            m, lo = divmod(made[0], 14)
            take = min(n, 14 - lo)
            make_signs_of(m, lo, lo + take)
            made[0] += take
            n -= take

    def rows_of(m, lo, n):
        return tc[m, pl.ds(lo, n)].reshape(n * BLOCK, D)

    def dir_body(i, _):
        acc[i] = lax.dot_general(rows_of(i // 4, 0, 4), dirs[i], NT, preferred_element_type=F32)
        return 0

    ag_send(0, 0)
    a2a_send(0, 1)
    a2a_send(0, 3)
    go(a2a_far(0))
    tz_open(0)
    tz_open(1)
    ag_send(1, 0)
    make_signs(15)
    ag_relay(0, 0)
    make_signs(6)
    for j in (1, 3):
        a2a_wait(0, j)
        ag_send(0, j)
    tz_pass(0)
    tz_pass(1)
    ag_relay(1, 0)
    make_signs(9)
    tz_half(0)
    tx_send(0, 1, 3)
    tz_half(1)
    go(a2a_far(1))
    make_signs(6)
    for j in (1, 3):
        ag_relay(0, j)
    tz_pass(2)
    tz_pass(3)
    for d in (1, 3, 2):
        a2a_send(1, d)
    make_signs(6)
    tz_rest(2)
    tx_send(0, 2)
    tx_relay(0, 1, 3)
    a2a_far_wait()
    ag_send(0, 2)
    tx_relay(0, 2)
    tx_send(1, 1, 3)
    ag_relay(0, 2)
    tok_share(0, 1, 3, 2)
    tz_rest(3)
    tx_send(1, 2)
    tok_finish(0)
    lax.fori_loop(0, 1, dir_body, 0)
    for j in (1, 3):
        a2a_wait(1, j)
        ag_send(1, j)
    tx_relay(1, 1, 3)
    lax.fori_loop(1, 3, dir_body, 0)
    a2a_wait(1, 2)
    ag_send(1, 2)
    tx_relay(1, 2)
    lax.fori_loop(3, 4, dir_body, 0)
    for j in (0, 1, 3, 2):
        ag_finish(0, j)

    def plain(i, _):
        rhs = jnp.concatenate([w[b % 4, b // 4, pl.ds(i * UNITS, UNITS), :] for b in range(16)], axis=1)
        acc[6 + i] = lax.dot_general(rows_of(i // 2, 0, 4), rhs, NT, preferred_element_type=F32)
        return 0

    lax.fori_loop(0, 2, plain, 0)
    for j in (1, 3):
        ag_relay(1, j)
    tok_share(1, 1, 3, 2)

    def point(i, _):
        r = pl.ds(pl.multiple_of(i * 32, 32), 32)
        gate, up = acc[6, r, :], acc[7, r, :]
        s = jax.nn.sigmoid(gate)
        silu = gate * s
        slope = s * (1.0 + gate * (1.0 - s))
        bend = s * (1.0 - s) * (2.0 + gate * (1.0 - 2.0 * s))
        hid[2, r, :] = (silu * up).astype(BF16)
        for p in range(2):
            gd, ud = acc[p, r, :] * IN_FACTOR, acc[2 + p, r, :] * IN_FACTOR
            hd = slope * gd * up + silu * ud
            hid[p, r, :] = hd.astype(BF16)
            acc[2 + p, r, :] = hd
            acc[p, r, :] = bend * gd * gd * up + 2.0 * slope * gd * ud
        return 0

    lax.fori_loop(0, 16, point, 0)
    ag_relay(1, 2)
    tok_finish(1)
    lax.fori_loop(4, 6, dir_body, 0)
    for j in (0, 1, 3, 2):
        ag_finish(1, j)

    def curvature_terms():
        cv[0] = jnp.zeros((8, 4 * BLOCK), F32)
        for p in range(2):
            terms = acc[8] * acc[p] + (2.0 * OUT_FACTOR_LOW) * acc[4 + p] * acc[2 + p]
            cv[0, pl.ds(p, 1), :] = jnp.sum(terms.T, axis=0, keepdims=True) * OUT_FACTOR
        go(remote(cv.at[0], cvc, vc_s.at[0], vc_r.at[0], dev_c))

    def columns(e, lr, other):
        return (((zl + lr) % 2) * 4 + (x + e) % 4) * 2 + other

    def tangent(p, b):
        col = pl.ds(pl.multiple_of(b * COLS, COLS), COLS)
        one = jnp.dot(hid[p], w[b % 4, b // 4, pl.ds(2 * UNITS, UNITS), :], preferred_element_type=F32)
        two = jnp.dot(hid[2], dirs[4 + p, :, col], preferred_element_type=F32)
        return one + two * OUT_FACTOR_LOW

    def column(p, g, i, side):
        return columns((i - x) % 4, g, side) if p else columns(g, i, side)

    def give(p, g):
        out_ref, in_ref = (cs1, cr1) if p else (cs0, cr0)
        return remote(out_ref.at[g], in_ref.at[g], c_s.at[p, g], c_r.at[p, g], dev_c)

    def theirs(p, g):
        n, out_ref = (4, cs1) if p else (2, cs0)

        def body(i, _):
            out_ref[g, pl.ds(i, 1)] = tangent(p, column(p, g, i, 1 - core)).astype(BF16)[None]
            return 0

        lax.fori_loop(0, n, body, 0)
        go(give(p, g))

    def ours(p, g):
        n, mine, in_ref = (4, s1, cr1) if p else (2, s0, cr0)
        give(p, g).wait_recv()

        def body(i, _):
            total = tangent(p, column(p, g, i, core)) + in_ref[g, i].astype(F32)
            mine[g, pl.ds(i, 1)] = total.astype(BF16)[None]
            return 0

        lax.fori_loop(0, n, body, 0)

    def z_rows(d, u):
        return pl.ds(pl.multiple_of((((zh * 2 + zl + d) % 8) // 2) * BLOCK + u * 64, 64), 64)

    def z_part(p, up, u, d):
        far = d if up else 8 - d
        rows = z_rows(far, u)
        return s1.at[far % 2, :, rows] if p else s0.at[0, pl.ds(far % 2, 1), rows]

    def z_hop(p, up, u, d):
        side = 0 if up else 1
        land = (zr1 if p else zr0).at[side, u, d - 1]
        return remote(
            z_part(p, up, u, d), land, z_s.at[p, side, u, d - 1], z_r.at[p, side, u, d - 1], dev_z(1 if up else 7)
        )

    def z_add(p, up, u, d):
        z_hop(p, up, u, d).wait_recv()
        far = (d - 1 if up else 9 - d) % 8
        side, r = 0 if up else 1, z_rows(far, u)
        if p:

            def body(i, _):
                s1[far % 2, i, r, :] = (s1[far % 2, i, r, :].astype(F32) + zr1[side, u, d - 1, i].astype(F32)).astype(BF16)
                return 0

            lax.fori_loop(0, 4, body, 0)
        else:
            s0[0, far % 2, r, :] = (s0[0, far % 2, r, :].astype(F32) + zr0[side, u, d - 1, 0].astype(F32)).astype(BF16)

    def z_open(p, d):
        go(z_hop(p, True, 4 - d, d))
        go(z_hop(p, False, d - 3, d))

    def z_lead(p, d):
        for up in (True, False):
            lane = 0 if up else 1
            z_add(p, up, lane, d + 1)
            go(z_hop(p, up, lane, d))

    def z_lag(p, d):
        for up in (True, False):
            lane = 1 if up else 0
            z_add(p, up, lane, d + 1)
            go(z_hop(p, up, lane, d))

    def z_end(p):
        for up in (True, False):
            for u in range(2):
                z_add(p, up, u, 1)

    def x_hop(up, u, d):
        side = 0 if up else 1
        e = d if up else 4 - d
        return remote(s0.at[e, u], xr0.at[side, u, d - 1], x0_s.at[side, u, d - 1], x0_r.at[side, u, d - 1], dev_x(1 if up else 3))

    def x_add(up, u, d):
        x_hop(up, u, d).wait_recv()
        e = (d - 1 if up else 5 - d) % 4

        def body(i, _):
            r = pl.ds(pl.multiple_of(i * 64, 64), 64)
            s0[e, u, r, :] = (s0[e, u, r, :].astype(F32) + xr0[0 if up else 1, u, d - 1, r, :].astype(F32)).astype(BF16)
            return 0

        lax.fori_loop(0, 8, body, 0)

    theirs(0, 2)
    theirs(1, 0)
    ours(0, 2)
    go(x_hop(True, 0, 2))
    go(x_hop(False, 1, 2))
    theirs(1, 1)
    ours(1, 0)
    z_open(1, 4)
    theirs(0, 1)
    ours(1, 1)
    z_open(1, 3)
    theirs(0, 3)
    ours(0, 1)
    go(x_hop(True, 1, 1))
    ours(0, 3)
    go(x_hop(False, 0, 1))
    x_add(True, 0, 2)
    go(x_hop(True, 0, 1))
    x_add(False, 1, 2)
    go(x_hop(False, 1, 1))
    theirs(0, 0)
    z_lead(1, 3)
    ours(0, 0)
    z_lag(1, 2)
    lax.fori_loop(2, 3, plain, 0)
    z_lead(1, 2)
    z_lag(1, 1)
    curvature_terms()
    z_lead(1, 1)
    for lr in range(2):
        x_add(True, lr, 1)
        x_add(False, lr, 1)
    z_open(0, 4)
    z_open(0, 3)
    remote(cvc, cvc, vc_s.at[0], vc_r.at[0], dev_c).wait_recv()
    cv[1] = cv[0] + cvc[...]
    for d in range(1, 4):
        go(remote(cv.at[1], cvx.at[d - 1], vx_s.at[d - 1], vx_r.at[d - 1], dev_x(d)))
    z_end(1)
    z_lead(0, 3)

    def x_copy(e):
        return remote(
            s1.at[0, (x + e) % 4, pl.ds(pl.multiple_of(zh * BLOCK, BLOCK), BLOCK)], xr1.at[e - 1], x1_s.at[e - 1], x1_r.at[e - 1], dev_x(e)
        )

    for e in range(1, 4):
        go(x_copy(e))
    z_lag(0, 2)
    z_lead(0, 2)
    for d in range(1, 4):
        remote(cv.at[1], cvx.at[d - 1], vx_s.at[d - 1], vx_r.at[d - 1], dev_x(d)).wait_recv()
    cv[2] = (cv[1] + cvx[0]) + (cvx[1] + cvx[2])
    for d in range(1, 8):
        zz = ((zh * 2 + zl + d) % 8) // 2
        src = cv.at[2, :, pl.ds(pl.multiple_of(zz * BLOCK, BLOCK), BLOCK)]
        go(remote(src, cvz.at[d - 1], vz_s.at[d - 1], vz_r.at[d - 1], dev_z(d)))
    z_lag(0, 1)
    z_lead(0, 1)

    for d in range(1, 8):
        remote(cvz.at[d - 1], cvz.at[d - 1], vz_s.at[d - 1], vz_r.at[d - 1], dev_z(d)).wait_recv()
    total = cv[2, :, pl.ds(pl.multiple_of(zh * BLOCK, BLOCK), BLOCK)]
    for d in range(7):
        total = total + cvz[d]
    curv[...] = total[:2]

    z_end(0)
    for e in range(1, 4):
        x_copy(e).wait_recv()

    def last(i, _):
        r = pl.ds(pl.multiple_of(i * 32, 32), 32)
        own = pl.ds(pl.multiple_of(zh * BLOCK + i * 32, 32), 32)
        out[0, r, :] = s0[0, 0, own, :]
        total = s1[0, x, own, :].astype(F32)
        for e in range(3):
            total = total + xr1[e, r, :].astype(F32)
        out[1, r, :] = total.astype(BF16)
        return 0

    lax.fori_loop(0, 4, last, 0)
    for up in (True, False):
        for k in range(4):
            tz(up, k, tz_block(up, k)).wait_send()
    for copy in started:
        copy.wait_send()


def on_device(tokens, cotangent, gate_weight, up_weight, down_weight, probe_seeds):
    dma = pltpu.SemaphoreType.DMA
    vmem = pltpu.VMEM
    hbm = pl.BlockSpec(memory_space=pl.ANY)
    tangent, curvature = pl.pallas_call(
        kernel,
        out_shape=(
            jax.ShapeDtypeStruct((2, BLOCK, COLS), BF16),
            jax.ShapeDtypeStruct((2, BLOCK), F32),
        ),
        in_specs=[pl.BlockSpec(memory_space=pltpu.SMEM), hbm, hbm, hbm, hbm, hbm],
        out_specs=(pl.BlockSpec(memory_space=pltpu.VMEM), pl.BlockSpec(memory_space=pltpu.VMEM)),
        scratch_shapes=[
            vmem((2, COLS, 4 * UNITS), BF16),
            vmem((4, 3 * UNITS, COLS), BF16),
            vmem((2, 4, 4, 2, 16, D), BF16),
            vmem((4, 4, 3 * UNITS, COLS), BF16),
            vmem((6, UNITS, D), BF16),
            vmem((9, 4 * BLOCK, UNITS), F32),
            vmem((3, 4 * BLOCK, UNITS), BF16),
            vmem((4, 2, 4 * BLOCK, COLS), BF16),
            vmem((4, 2, 4 * BLOCK, COLS), BF16),
            vmem((4, 2, 4 * BLOCK, COLS), BF16),
            vmem((2, 2, 2, 4 * BLOCK, COLS), BF16),
            vmem((2, 2, 4, 1, 64, COLS), BF16),
            vmem((2, 4, 4 * BLOCK, COLS), BF16),
            vmem((2, 4, 4 * BLOCK, COLS), BF16),
            vmem((2, 4, 4 * BLOCK, COLS), BF16),
            vmem((2, 2, 4, 4, 64, COLS), BF16),
            vmem((3, BLOCK, COLS), BF16),
            vmem((3, 8, 4 * BLOCK), F32),
            vmem((8, 4 * BLOCK), F32),
            vmem((3, 8, 4 * BLOCK), F32),
            vmem((7, 8, BLOCK), F32),
            dma((5,)),
            dma((2, 4)), dma((2, 4)),
            dma((2, 4, 3)), dma((2, 4, 3)),
            dma((2, 4)), dma((2, 4)),
            dma((3, 2, 4)), dma((3, 2, 4)),
            dma((2, 3)), dma((2, 3)),
            dma((2, 4)), dma((2, 4)),
            dma((2, 2, 2)), dma((2, 2, 2)),
            dma((2, 2, 2, 4)), dma((2, 2, 2, 4)),
            dma((3,)), dma((3,)),
            dma((1,)), dma((1,)),
            dma((3,)), dma((3,)),
            dma((7,)), dma((7,)),
        ],
        name="curvature_probes",
        cost_estimate=pl.CostEstimate(flops=13 * 2 * 512 * D * UNITS, bytes_accessed=4 * 2**20, transcendentals=512 * UNITS),
        compiler_params=pltpu.CompilerParams(
            collective_id=0, has_side_effects=True, vmem_limit_bytes=60 * 2**20
        ),
    )(
        probe_seeds,
        tokens.reshape(4, 2, 16, D),
        cotangent.reshape(4, 2, 16, D),
        gate_weight,
        up_weight,
        down_weight.reshape(4, UNITS, COLS),
    )
    return tangent, curvature


def solution(mesh):
    return jax.shard_map(
        on_device,
        mesh=mesh,
        in_specs=(
            P("dp", None),
            P("dp", None),
            P("dp", ("tensor", "probe")),
            P("dp", ("tensor", "probe")),
            P(("tensor", "probe"), "dp"),
            P(),
        ),
        out_specs=(P(None, "dp", ("tensor", "probe")), P(None, "dp")),
        check_vma=False,
    )
```

```python
import functools

import jax
import jax.numpy as jnp
import numpy as np
from jax import lax
from jax.experimental import pallas as pl
from jax.experimental.pallas import tpu as pltpu
from jax.sharding import PartitionSpec as P

D = 4096
FF = 14336
UNITS = 224
COLS = 256
BLOCK = 128
MESH = pl.DeviceIdType.MESH
NT = (((1,), (1,)), ((), ()))
BF16, F32, I32 = jnp.bfloat16, jnp.float32, jnp.int32
IN_FACTOR = float(D**-0.5)
OUT_FACTOR = float(FF**-0.5)
OUT_FACTOR_LOW = float(np.asarray(FF**-0.5, np.float32).astype(jnp.bfloat16))
PARTS = ((0, 2 * UNITS), (2 * UNITS, UNITS))


def wrap(value):
    return np.int32((int(value) + 2**31) % 2**32 - 2**31)


STEP = -1640531535


def kernel(
    seeds, tok, cot, gate, up, down, out, curv,
    wide, wa, tc, w, dirs, acc, hid, cs0, cr0, s0, xr0, zr0, cs1, cr1, s1, zr1, xr1, cv, cvc, cvx, cvz,
    loc_sem, a2a_s, a2a_r, ag_s, ag_r, tz_s, tz_r, tx_s, tx_r, tcc_s, tcc_r,
    c_s, c_r, x0_s, x0_r, z_s, z_r, x1_s, x1_r, vc_s, vc_r, vx_s, vx_r, vz_s, vz_r,
):
    dp, tensor, core = lax.axis_index("dp"), lax.axis_index("tensor"), lax.axis_index("probe")
    zh, y = dp // 4, dp % 4
    zl, x = tensor // 4, tensor % 4

    def dev_z(step):
        z = (zh * 2 + zl + step) % 8
        return ((z // 2) * 4 + y, (z % 2) * 4 + x, core)

    def dev_y(step):
        return (zh * 4 + (y + step) % 4, tensor, core)

    def dev_x(step):
        return (dp, zl * 4 + (x + step) % 4, core)

    dev_c = (dp, tensor, 1 - core)

    def remote(src, dst, send, recv, device):
        return pltpu.make_async_remote_copy(
            src_ref=src, dst_ref=dst, send_sem=send, recv_sem=recv,
            device_id=device, device_id_type=MESH,
        )

    barrier = pltpu.get_barrier_semaphore()
    peers = [dev_z(d) for d in range(1, 8)] + [dev_x(d) for d in range(1, 4)] + [dev_y(1), dev_y(3), dev_c]
    for peer in peers:
        pl.semaphore_signal(barrier, inc=1, device_id=peer, device_id_type=MESH)
    local = [
        pltpu.make_async_copy(tok, tc.at[0, zh], loc_sem.at[0]),
        pltpu.make_async_copy(cot, tc.at[1, zh], loc_sem.at[1]),
        pltpu.make_async_copy(down, wa.at[:, pl.ds(2 * UNITS, UNITS)], loc_sem.at[2]),
        pltpu.make_async_copy(gate, wide.at[0], loc_sem.at[3]),
        pltpu.make_async_copy(up, wide.at[1], loc_sem.at[4]),
    ]
    for k in (3, 4, 2, 0, 1):
        local[k].start()
    for k in range(2):
        local[3 + k].wait()
        wa[:, pl.ds(k * UNITS, UNITS), :] = wide[k].T.reshape(4, UNITS, COLS)
    local[2].wait()
    w[y, zh] = wa[zh]
    pl.semaphore_wait(barrier, len(peers))

    started = []

    def go(copy):
        copy.start()
        started.append(copy)

    def w_at(part, yy, j):
        lo, n = PARTS[part]
        return w.at[yy % 4, (zh + j) % 4, pl.ds(lo, n)]

    def ag_send(part, j):
        lo, n = PARTS[part]
        src = wa.at[zh, pl.ds(lo, n)] if j == 0 else w_at(part, y, j)
        go(remote(src, w_at(part, y, j), ag_s.at[part, j, 0], ag_r.at[part, j, 0], dev_y(1)))
        go(remote(src, w_at(part, y, j), ag_s.at[part, j, 1], ag_r.at[part, j, 1], dev_y(3)))

    def ag_wait(part, j, side, source):
        ref = w_at(part, source, j)
        remote(ref, ref, ag_s.at[part, j, side], ag_r.at[part, j, side], dev_y(1)).wait_recv()

    def ag_relay(part, j):
        side, source, onward = (0, y + 3, 1) if j % 2 == 0 else (1, y + 1, 3)
        ag_wait(part, j, side, source)
        ref = w_at(part, source, j)
        go(remote(ref, ref, ag_s.at[part, j, 2], ag_r.at[part, j, 2], dev_y(onward)))

    def ag_finish(part, j):
        side, source = (1, y + 1) if j % 2 == 0 else (0, y + 3)
        ag_wait(part, j, side, source)
        ag_wait(part, j, 2, y + 2)

    def a2a_send(part, d):
        lo, n = PARTS[part]
        target = (zh + d) % 4
        go(remote(wa.at[target, pl.ds(lo, n)], w_at(part, y, 0), a2a_s.at[part, d - 1], a2a_r.at[part, 3 - d], dev_z(2 * d)))

    def a2a_far(k):
        rows = pl.ds(k * UNITS, UNITS)
        return remote(
            wa.at[(zh + 2) % 4, rows], w.at[y, zh, rows], a2a_s.at[0, 1 + 2 * k], a2a_r.at[0, 1 + 2 * k], dev_z(4)
        )

    def a2a_far_wait():
        for k in range(2):
            a2a_far(k).wait_recv()

    def a2a_wait(part, j):
        ref = w_at(part, y, j)
        remote(ref, ref, a2a_s.at[part, j - 1], a2a_r.at[part, j - 1], dev_z(2)).wait_recv()

    HALF = (pl.ds(0, D // 2), pl.ds(D // 2, D // 2))

    def tz(up, k, block, own=False):
        side, m = 0 if up else 1, k % 2
        dst = tc.at[m, block % 4, x, core]
        src = (tok, cot)[m].at[x, core] if own else dst
        if k > 1:
            dst = dst.at[:, HALF[side]]
            src = dst
        return remote(src, dst, tz_s.at[side, k], tz_r.at[side, k], dev_z(1 if up else 7))

    def tz_block(up, k):
        return zh + 2 if k > 1 else zh + 3 if up else zh + 1

    def tz_wait(up, k):
        tz(up, k, tz_block(up, k)).wait_recv()

    def tz_open(k):
        for up in (True, False):

            @pl.when(zl == (1 if up else 0))
            def _():
                tz(up, k, zh, own=True).start()

    def tz_pass(k):
        for up in (True, False):

            @pl.when(zl == (0 if up else 1))
            def _():
                tz_wait(up, k)
                tz(up, k, tz_block(up, k)).start()

    def tz_half(m):
        for up in (True, False):

            @pl.when(zl == (1 if up else 0))
            def _():
                tz_wait(up, m)
                tz(up, m + 2, tz_block(up, m)).start()

    def tz_rest(k):
        for up in (True, False):

            @pl.when(zl == (1 if up else 0))
            def _():
                tz_wait(up, k)

    def tx(j, m, side, source=0):
        ref = tc.at[m, (zh + j) % 4, (x + source) % 4, core]
        return remote(ref, ref, tx_s.at[j - 1, m, side], tx_r.at[j - 1, m, side], dev_x(1 if side == 0 else 3))

    def tx_onward(j, m, side, source):
        ref = tc.at[m, (zh + j) % 4, (x + source) % 4, core, :, HALF[side]]
        return remote(ref, ref, tx_s.at[j - 1, m, 2 + side], tx_r.at[j - 1, m, 2 + side], dev_x(1 if side == 0 else 3))

    def tx_send(m, *js):
        for j in js:
            go(tx(j, m, 0))
            go(tx(j, m, 1))

    def tx_relay(m, *js):
        for j in js:
            for side, source in ((0, 3), (1, 1)):
                tx(j, m, side, source).wait_recv()
                go(tx_onward(j, m, side, source))

    def tok_share(m, *js):
        for j in js:
            for side in range(2):
                tx_onward(j, m, side, 2).wait_recv()
            ref = tc.at[m, (zh + j) % 4, :, core]
            go(remote(ref, ref, tcc_s.at[m, j - 1], tcc_r.at[m, j - 1], dev_c))

    def tok_finish(m):
        for j in (1, 3, 2):
            ref = tc.at[m, (zh + j) % 4, :, 1 - core]
            remote(ref, ref, tcc_s.at[m, j - 1], tcc_r.at[m, j - 1], dev_c).wait_recv()
        local[m].wait()

    first_unit = (tensor * 2 + core) * (4 * UNITS) + zh * UNITS

    def make_signs_of(m, lo, hi):
        unit_mul, feature_mul = (wrap(STEP), wrap(STEP * FF)) if m < 2 else (wrap(STEP * D), wrap(STEP))
        base = (
            lax.broadcasted_iota(I32, (16, D), 0) * unit_mul + lax.broadcasted_iota(I32, (16, D), 1) * feature_mul
        )

        def body(i, _):
            start = (first_unit + i * 16) * unit_mul + np.int32(40503 * (m + 1))
            for p in range(2):
                u = base + (start + seeds[p])
                u = u ^ lax.shift_right_logical(u, np.int32(16))
                u = u * np.int32(739982445)
                u = u ^ lax.shift_right_logical(u, np.int32(13))
                u = u * np.int32(695872825)
                dirs[2 * m + p, pl.ds(pl.multiple_of(i * 16, 16), 16), :] = jnp.where(u < 0, -1.0, 1.0).astype(BF16)
            return 0

        lax.fori_loop(lo, hi, body, 0)

    made = [0]

    def make_signs(n):
        while n:
            m, lo = divmod(made[0], 14)
            take = min(n, 14 - lo)
            make_signs_of(m, lo, lo + take)
            made[0] += take
            n -= take

    def rows_of(m, lo, n):
        return tc[m, pl.ds(lo, n)].reshape(n * BLOCK, D)

    def dir_body(i, _):
        acc[i] = lax.dot_general(rows_of(i // 4, 0, 4), dirs[i], NT, preferred_element_type=F32)
        return 0

    ag_send(0, 0)
    a2a_send(0, 1)
    a2a_send(0, 3)
    go(a2a_far(0))
    tz_open(0)
    tz_open(1)
    ag_send(1, 0)
    make_signs(15)
    ag_relay(0, 0)
    make_signs(6)
    for j in (1, 3):
        a2a_wait(0, j)
        ag_send(0, j)
    tz_pass(0)
    tz_pass(1)
    ag_relay(1, 0)
    make_signs(9)
    tz_half(0)
    tx_send(0, 1, 3)
    tz_half(1)
    go(a2a_far(1))
    make_signs(6)
    for j in (1, 3):
        ag_relay(0, j)
    tz_pass(2)
    tz_pass(3)
    for d in (2, 1, 3):
        a2a_send(1, d)
    make_signs(6)
    tz_rest(2)
    tx_send(0, 2)
    tx_relay(0, 1, 3)
    a2a_far_wait()
    ag_send(0, 2)
    tx_relay(0, 2)
    tx_send(1, 1, 3)
    ag_relay(0, 2)
    tok_share(0, 1, 3, 2)
    tz_rest(3)
    tx_send(1, 2)
    tok_finish(0)
    lax.fori_loop(0, 1, dir_body, 0)
    for j in (1, 3):
        a2a_wait(1, j)
        ag_send(1, j)
    tx_relay(1, 1, 3)
    lax.fori_loop(1, 3, dir_body, 0)
    a2a_wait(1, 2)
    ag_send(1, 2)
    tx_relay(1, 2)
    lax.fori_loop(3, 4, dir_body, 0)
    for j in (0, 1, 3, 2):
        ag_finish(0, j)

    def plain(i, _):
        rhs = jnp.concatenate([w[b % 4, b // 4, pl.ds(i * UNITS, UNITS), :] for b in range(16)], axis=1)
        acc[6 + i] = lax.dot_general(rows_of(i // 2, 0, 4), rhs, NT, preferred_element_type=F32)
        return 0

    lax.fori_loop(0, 2, plain, 0)
    for j in (1, 3):
        ag_relay(1, j)
    tok_share(1, 1, 3, 2)

    def point(i, _):
        r = pl.ds(pl.multiple_of(i * 32, 32), 32)
        gate, up = acc[6, r, :], acc[7, r, :]
        s = jax.nn.sigmoid(gate)
        silu = gate * s
        slope = s * (1.0 + gate * (1.0 - s))
        bend = s * (1.0 - s) * (2.0 + gate * (1.0 - 2.0 * s))
        hid[2, r, :] = (silu * up).astype(BF16)
        for p in range(2):
            gd, ud = acc[p, r, :] * IN_FACTOR, acc[2 + p, r, :] * IN_FACTOR
            hd = slope * gd * up + silu * ud
            hid[p, r, :] = hd.astype(BF16)
            acc[2 + p, r, :] = hd
            acc[p, r, :] = bend * gd * gd * up + 2.0 * slope * gd * ud
        return 0

    lax.fori_loop(0, 16, point, 0)
    ag_relay(1, 2)
    tok_finish(1)
    lax.fori_loop(4, 6, dir_body, 0)
    for j in (0, 1, 3, 2):
        ag_finish(1, j)

    def curvature_terms():
        cv[0] = jnp.zeros((8, 4 * BLOCK), F32)
        for p in range(2):
            terms = acc[8] * acc[p] + (2.0 * OUT_FACTOR_LOW) * acc[4 + p] * acc[2 + p]
            cv[0, pl.ds(p, 1), :] = jnp.sum(terms.T, axis=0, keepdims=True) * OUT_FACTOR
        go(remote(cv.at[0], cvc, vc_s.at[0], vc_r.at[0], dev_c))

    def columns(e, lr, other):
        return (((zl + lr) % 2) * 4 + (x + e) % 4) * 2 + other

    def tangent(p, b):
        col = pl.ds(pl.multiple_of(b * COLS, COLS), COLS)
        one = jnp.dot(hid[p], w[b % 4, b // 4, pl.ds(2 * UNITS, UNITS), :], preferred_element_type=F32)
        two = jnp.dot(hid[2], dirs[4 + p, :, col], preferred_element_type=F32)
        return one + two * OUT_FACTOR_LOW

    def column(p, g, i, side):
        return columns((i - x) % 4, g, side) if p else columns(g, i, side)

    def give(p, g):
        out_ref, in_ref = (cs1, cr1) if p else (cs0, cr0)
        return remote(out_ref.at[g], in_ref.at[g], c_s.at[p, g], c_r.at[p, g], dev_c)

    def theirs(p, g):
        n, out_ref = (4, cs1) if p else (2, cs0)

        def body(i, _):
            out_ref[g, pl.ds(i, 1)] = tangent(p, column(p, g, i, 1 - core)).astype(BF16)[None]
            return 0

        lax.fori_loop(0, n, body, 0)
        go(give(p, g))

    def ours(p, g):
        n, mine, in_ref = (4, s1, cr1) if p else (2, s0, cr0)
        give(p, g).wait_recv()

        def body(i, _):
            total = tangent(p, column(p, g, i, core)) + in_ref[g, i].astype(F32)
            mine[g, pl.ds(i, 1)] = total.astype(BF16)[None]
            return 0

        lax.fori_loop(0, n, body, 0)

    def z_rows(d, u):
        return pl.ds(pl.multiple_of((((zh * 2 + zl + d) % 8) // 2) * BLOCK + u * 64, 64), 64)

    def z_part(p, up, u, d):
        far = d if up else 8 - d
        rows = z_rows(far, u)
        return s1.at[far % 2, :, rows] if p else s0.at[0, pl.ds(far % 2, 1), rows]

    def z_hop(p, up, u, d):
        side = 0 if up else 1
        land = (zr1 if p else zr0).at[side, u, d - 1]
        return remote(
            z_part(p, up, u, d), land, z_s.at[p, side, u, d - 1], z_r.at[p, side, u, d - 1], dev_z(1 if up else 7)
        )

    def z_add(p, up, u, d):
        z_hop(p, up, u, d).wait_recv()
        far = (d - 1 if up else 9 - d) % 8
        side, r = 0 if up else 1, z_rows(far, u)
        if p:

            def body(i, _):
                s1[far % 2, i, r, :] = (s1[far % 2, i, r, :].astype(F32) + zr1[side, u, d - 1, i].astype(F32)).astype(BF16)
                return 0

            lax.fori_loop(0, 4, body, 0)
        else:
            s0[0, far % 2, r, :] = (s0[0, far % 2, r, :].astype(F32) + zr0[side, u, d - 1, 0].astype(F32)).astype(BF16)

    def z_open(p, d):
        go(z_hop(p, True, 4 - d, d))
        go(z_hop(p, False, d - 3, d))

    def z_lead(p, d):
        for up in (True, False):
            lane = 0 if up else 1
            z_add(p, up, lane, d + 1)
            go(z_hop(p, up, lane, d))

    def z_lag(p, d):
        for up in (True, False):
            lane = 1 if up else 0
            z_add(p, up, lane, d + 1)
            go(z_hop(p, up, lane, d))

    def z_end(p):
        for up in (True, False):
            for u in range(2):
                z_add(p, up, u, 1)

    def x_hop(up, u, d):
        side = 0 if up else 1
        e = d if up else 4 - d
        return remote(s0.at[e, u], xr0.at[side, u, d - 1], x0_s.at[side, u, d - 1], x0_r.at[side, u, d - 1], dev_x(1 if up else 3))

    def x_add(up, u, d):
        x_hop(up, u, d).wait_recv()
        e = (d - 1 if up else 5 - d) % 4

        def body(i, _):
            r = pl.ds(pl.multiple_of(i * 64, 64), 64)
            s0[e, u, r, :] = (s0[e, u, r, :].astype(F32) + xr0[0 if up else 1, u, d - 1, r, :].astype(F32)).astype(BF16)
            return 0

        lax.fori_loop(0, 8, body, 0)

    theirs(0, 2)
    theirs(1, 0)
    ours(0, 2)
    go(x_hop(True, 0, 2))
    go(x_hop(False, 1, 2))
    theirs(1, 1)
    ours(1, 0)
    z_open(1, 4)
    theirs(0, 1)
    ours(1, 1)
    z_open(1, 3)
    theirs(0, 3)
    ours(0, 1)
    go(x_hop(True, 1, 1))
    ours(0, 3)
    go(x_hop(False, 0, 1))
    x_add(True, 0, 2)
    go(x_hop(True, 0, 1))
    x_add(False, 1, 2)
    go(x_hop(False, 1, 1))
    theirs(0, 0)
    z_lead(1, 3)
    ours(0, 0)
    z_lag(1, 2)
    lax.fori_loop(2, 3, plain, 0)
    z_lead(1, 2)
    z_lag(1, 1)
    curvature_terms()
    z_lead(1, 1)
    for lr in range(2):
        x_add(True, lr, 1)
        x_add(False, lr, 1)
    z_open(0, 4)
    z_open(0, 3)
    remote(cvc, cvc, vc_s.at[0], vc_r.at[0], dev_c).wait_recv()
    cv[1] = cv[0] + cvc[...]
    for d in range(1, 4):
        go(remote(cv.at[1], cvx.at[d - 1], vx_s.at[d - 1], vx_r.at[d - 1], dev_x(d)))
    z_end(1)
    z_lead(0, 3)

    def x_copy(e):
        return remote(
            s1.at[0, (x + e) % 4, pl.ds(pl.multiple_of(zh * BLOCK, BLOCK), BLOCK)], xr1.at[e - 1], x1_s.at[e - 1], x1_r.at[e - 1], dev_x(e)
        )

    for e in range(1, 4):
        go(x_copy(e))
    z_lag(0, 2)
    z_lead(0, 2)
    for d in range(1, 4):
        remote(cv.at[1], cvx.at[d - 1], vx_s.at[d - 1], vx_r.at[d - 1], dev_x(d)).wait_recv()
    cv[2] = (cv[1] + cvx[0]) + (cvx[1] + cvx[2])
    for d in range(1, 8):
        zz = ((zh * 2 + zl + d) % 8) // 2
        src = cv.at[2, :, pl.ds(pl.multiple_of(zz * BLOCK, BLOCK), BLOCK)]
        go(remote(src, cvz.at[d - 1], vz_s.at[d - 1], vz_r.at[d - 1], dev_z(d)))
    z_lag(0, 1)
    z_lead(0, 1)

    for d in range(1, 8):
        remote(cvz.at[d - 1], cvz.at[d - 1], vz_s.at[d - 1], vz_r.at[d - 1], dev_z(d)).wait_recv()
    total = cv[2, :, pl.ds(pl.multiple_of(zh * BLOCK, BLOCK), BLOCK)]
    for d in range(7):
        total = total + cvz[d]
    curv[...] = total[:2]

    z_end(0)
    for e in range(1, 4):
        x_copy(e).wait_recv()

    def last(i, _):
        r = pl.ds(pl.multiple_of(i * 32, 32), 32)
        own = pl.ds(pl.multiple_of(zh * BLOCK + i * 32, 32), 32)
        out[0, r, :] = s0[0, 0, own, :]
        total = s1[0, x, own, :].astype(F32)
        for e in range(3):
            total = total + xr1[e, r, :].astype(F32)
        out[1, r, :] = total.astype(BF16)
        return 0

    lax.fori_loop(0, 4, last, 0)
    for up in (True, False):
        for k in range(4):
            tz(up, k, tz_block(up, k)).wait_send()
    for copy in started:
        copy.wait_send()


def on_device(tokens, cotangent, gate_weight, up_weight, down_weight, probe_seeds):
    dma = pltpu.SemaphoreType.DMA
    vmem = pltpu.VMEM
    hbm = pl.BlockSpec(memory_space=pl.ANY)
    tangent, curvature = pl.pallas_call(
        kernel,
        out_shape=(
            jax.ShapeDtypeStruct((2, BLOCK, COLS), BF16),
            jax.ShapeDtypeStruct((2, BLOCK), F32),
        ),
        in_specs=[pl.BlockSpec(memory_space=pltpu.SMEM), hbm, hbm, hbm, hbm, hbm],
        out_specs=(pl.BlockSpec(memory_space=pltpu.VMEM), pl.BlockSpec(memory_space=pltpu.VMEM)),
        scratch_shapes=[
            vmem((2, COLS, 4 * UNITS), BF16),
            vmem((4, 3 * UNITS, COLS), BF16),
            vmem((2, 4, 4, 2, 16, D), BF16),
            vmem((4, 4, 3 * UNITS, COLS), BF16),
            vmem((6, UNITS, D), BF16),
            vmem((9, 4 * BLOCK, UNITS), F32),
            vmem((3, 4 * BLOCK, UNITS), BF16),
            vmem((4, 2, 4 * BLOCK, COLS), BF16),
            vmem((4, 2, 4 * BLOCK, COLS), BF16),
            vmem((4, 2, 4 * BLOCK, COLS), BF16),
            vmem((2, 2, 2, 4 * BLOCK, COLS), BF16),
            vmem((2, 2, 4, 1, 64, COLS), BF16),
            vmem((2, 4, 4 * BLOCK, COLS), BF16),
            vmem((2, 4, 4 * BLOCK, COLS), BF16),
            vmem((2, 4, 4 * BLOCK, COLS), BF16),
            vmem((2, 2, 4, 4, 64, COLS), BF16),
            vmem((3, BLOCK, COLS), BF16),
            vmem((3, 8, 4 * BLOCK), F32),
            vmem((8, 4 * BLOCK), F32),
            vmem((3, 8, 4 * BLOCK), F32),
            vmem((7, 8, BLOCK), F32),
            dma((5,)),
            dma((2, 4)), dma((2, 4)),
            dma((2, 4, 3)), dma((2, 4, 3)),
            dma((2, 4)), dma((2, 4)),
            dma((3, 2, 4)), dma((3, 2, 4)),
            dma((2, 3)), dma((2, 3)),
            dma((2, 4)), dma((2, 4)),
            dma((2, 2, 2)), dma((2, 2, 2)),
            dma((2, 2, 2, 4)), dma((2, 2, 2, 4)),
            dma((3,)), dma((3,)),
            dma((1,)), dma((1,)),
            dma((3,)), dma((3,)),
            dma((7,)), dma((7,)),
        ],
        name="curvature_probes",
        cost_estimate=pl.CostEstimate(flops=13 * 2 * 512 * D * UNITS, bytes_accessed=4 * 2**20, transcendentals=512 * UNITS),
        compiler_params=pltpu.CompilerParams(
            collective_id=0, has_side_effects=True, vmem_limit_bytes=60 * 2**20
        ),
    )(
        probe_seeds,
        tokens.reshape(4, 2, 16, D),
        cotangent.reshape(4, 2, 16, D),
        gate_weight,
        up_weight,
        down_weight.reshape(4, UNITS, COLS),
    )
    return tangent, curvature


def solution(mesh):
    return jax.shard_map(
        on_device,
        mesh=mesh,
        in_specs=(
            P("dp", None),
            P("dp", None),
            P("dp", ("tensor", "probe")),
            P("dp", ("tensor", "probe")),
            P(("tensor", "probe"), "dp"),
            P(),
        ),
        out_specs=(P(None, "dp", ("tensor", "probe")), P(None, "dp")),
        check_vma=False,
    )
```
